256 devices in a mesh: comp: 32 (over y_hi, z, core), seq: 8 (over y_lo, x).
Axes of the slice: x: 4, y: 4 (y_hi: 2, y_lo: 2; y = y_hi * 2 + y_lo), z: 8, core: 2. Of those that a mesh axis runs over, the one named last changes fastest.
Arguments:
- comp_query: bfloat16 [32, 512, 16, 256], P('comp', None, 'seq'), may hold values from -180 to 180
- comp_key: bfloat16 [32, 512, 16, 256], P('comp', None, 'seq'), may hold values from -6 to 6
- comp_value: bfloat16 [32, 512, 16, 256], P('comp', None, 'seq'), may hold values from -6 to 6
- prompt_key: bfloat16 [512, 16, 256], P('seq'), may hold values from -7 to 7
- prompt_value: bfloat16 [512, 16, 256], P('seq'), may hold values from -6 to 6
- lam: float32 [16], P('seq'), may hold values from 0.2 to 0.8
- gain: float32 [16, 256], P('seq'), may hold values from 0.25 to 1.75
- cotangent: bfloat16 [32, 512, 16, 256], P('comp', None, 'seq'), may hold values from -6 to 6
- lengths: int32 [32], P('comp'), may hold values from 64 to 512, as said below
Outputs:
- grad_query: bfloat16 [32, 512, 16, 256], P('comp', None, 'seq')
- grad_key: bfloat16 [32, 512, 16, 256], P('comp', None, 'seq')
- grad_value: bfloat16 [32, 512, 16, 256], P('comp', None, 'seq')
- grad_prompt_key: bfloat16 [512, 16, 256], P(('comp', 'seq'))
- grad_prompt_value: bfloat16 [512, 16, 256], P(('comp', 'seq'))
The draws below stay inside these ranges and needn't reach their ends.
Inputs may be any that keep to these rules, and one draw needn't show every extreme that they name: `lengths`: some completion has all 512 tokens live.
All inputs are finite; a program needn't handle non-finite values.
Results may differ from the reference program's by a relative error of at most 0.017.
Values may be sent and summed in bfloat16 or wider, within the bound.
A program may use at most 64 MiB of HBM per device.

```python
import jax
import jax.numpy as jnp
from jax import lax

HEAD = 128
VDIM = 256
HEADS = 16
COMP_LEN = 512
COMPS = 32
PROMPT = 512


def shared_prompt(key):
    base = jax.random.truncated_normal(key, -6.0, 6.0, (PROMPT, HEADS, 2 * HEAD), jnp.float32)
    return base


def draw_prompt_key(key, part):
    base = shared_prompt(key)
    result = base
    return result.astype(jnp.bfloat16)


def draw_comp_query(key, part):
    key = jax.random.fold_in(key, 5)
    noise = jax.random.truncated_normal(key, -6.0, 6.0, (COMPS, COMP_LEN, HEADS, 2 * HEAD), jnp.float32)
    result = noise
    return result.astype(jnp.bfloat16)


def draw_lengths(key, part):
    key = jax.random.fold_in(key, 9)
    first_key, second_key = jax.random.split(key)
    values = jax.random.randint(first_key, (COMPS,), COMP_LEN // 8, COMP_LEN + 1, dtype=jnp.int32)
    longest = jax.random.randint(second_key, (), 0, COMPS, dtype=jnp.int32)
    return jnp.where(jnp.arange(COMPS, dtype=jnp.int32) == longest, COMP_LEN, values).astype(jnp.int32)


def steps_of(key, dims, cuts, least, high):
    level, own = 1.0, jax.random.fold_in(key, 6)
    for dim, shards_of in cuts:
        heights = jnp.exp(jax.random.uniform(jax.random.fold_in(own, dim), (shards_of,), jnp.float32, least / len(cuts), high / len(cuts)))
        level = level * jnp.repeat(heights, dims[dim] // shards_of).reshape([-1 if axis == dim else 1 for axis in range(len(dims))])
    return level


def scatter_about(own_key, shape, width, most, pieces=(), held_as=jnp.bfloat16):
    values = jax.random.normal(own_key, shape, jnp.float32) * width
    if len(pieces) > 0:
        values = steps_of(own_key, shape, pieces, -0.22, 0.18) * values
    return jnp.clip(values, min=-most, max=most).astype(held_as)


def setup_inputs(seed: int = 0) -> dict:
    seeds = jax.random.split(jax.random.key(seed), 10)
    comp_query = draw_comp_query(jax.random.fold_in(seeds[9], 71), 0)
    comp_key = scatter_about(seeds[1], (COMPS, COMP_LEN, HEADS, 2 * HEAD), 1.0, 6.0, ((0, 32), (2, 8)))
    comp_value = scatter_about(seeds[2], (COMPS, COMP_LEN, HEADS, VDIM), 1.0, 6.0, ((0, 32), (2, 8)))
    prompt_key = draw_prompt_key(jax.random.fold_in(seeds[9], 71), 0)
    prompt_value = scatter_about(seeds[4], (PROMPT, HEADS, VDIM), 1.0, 6.0, ((0, 8),))
    lam = jnp.clip(0.2 + 0.6 * jax.random.uniform(seeds[5], (HEADS,), jnp.float32) ** steps_of(seeds[5], (HEADS,), ((0, 8),), -0.2, 0.2), 0.2, 0.8)
    gain = jnp.clip(1.0 + 0.15 * jax.random.normal(seeds[6], (HEADS, VDIM), jnp.float32), 0.25, 1.75)
    cotangent = scatter_about(seeds[7], (COMPS, COMP_LEN, HEADS, VDIM), 1.0, 6.0, ((0, 32), (2, 8)))
    lengths = draw_lengths(jax.random.fold_in(seeds[9], 71), 0)
    return dict(comp_query=comp_query, comp_key=comp_key, comp_value=comp_value, prompt_key=prompt_key, prompt_value=prompt_value, lam=lam, gain=gain, cotangent=cotangent, lengths=lengths)


def head_terms(queries, all_keys, all_values, grad_out, weight_two, norm_gain, live_rows, visible):
    half_width = queries.shape[1] // 2
    score_scale = float(half_width) ** (-0.5)
    top = lax.Precision.HIGHEST
    query_f = queries.astype(jnp.float32)
    key_f = all_keys.astype(jnp.float32)
    value_f = all_values.astype(jnp.float32)
    first_query, second_query = (query_f[:, :half_width], query_f[:, half_width:])
    first_key, second_key = (key_f[:, :half_width], key_f[:, half_width:])

    def softmax_rows(scores):
        scores = jnp.where(visible, scores, -1e+30)
        peak = lax.optimization_barrier(jnp.max(scores, axis=1, keepdims=True))
        expo = jnp.exp(scores - peak)
        return expo / lax.optimization_barrier(jnp.sum(expo, axis=1, keepdims=True))
    map_one = softmax_rows(score_scale * jnp.dot(first_query, first_key.T, precision=top))
    map_two = softmax_rows(score_scale * jnp.dot(second_query, second_key.T, precision=top))
    mixed = (map_one - weight_two * map_two).astype(jnp.bfloat16)
    mixed_f = mixed.astype(jnp.float32)
    attn = jnp.dot(mixed_f, value_f, precision=top)
    recip = lax.rsqrt(lax.optimization_barrier(jnp.mean(attn * attn, axis=1, keepdims=True)) + 1e-05)
    normed_grad = jnp.where(live_rows[:, None], grad_out.astype(jnp.float32), 0.0) * norm_gain[None, :]
    inner = lax.optimization_barrier(jnp.mean(normed_grad * attn, axis=1, keepdims=True))
    d_attn = (recip * (normed_grad - attn * recip * recip * inner)).astype(jnp.bfloat16)
    d_attn_f = d_attn.astype(jnp.float32)
    d_mixed = jnp.dot(d_attn_f, value_f.T, precision=top)
    sum_one = lax.optimization_barrier(jnp.sum(map_one * d_mixed, axis=1, keepdims=True))
    sum_two = lax.optimization_barrier(jnp.sum(map_two * d_mixed, axis=1, keepdims=True))
    d_score_one = (map_one * (d_mixed - sum_one)).astype(jnp.bfloat16).astype(jnp.float32)
    d_score_two = (-weight_two * map_two * (d_mixed - sum_two)).astype(jnp.bfloat16).astype(jnp.float32)
    grad_q = score_scale * jnp.concatenate([jnp.dot(d_score_one, first_key, precision=top), jnp.dot(d_score_two, second_key, precision=top)], axis=1)
    grad_k = score_scale * jnp.concatenate([jnp.dot(d_score_one.T, first_query, precision=top), jnp.dot(d_score_two.T, second_query, precision=top)], axis=1)
    grad_v = jnp.dot(mixed_f.T, d_attn_f, precision=top)
    return (grad_q, grad_k, grad_v)

def reference(comp_query, comp_key, comp_value, prompt_key, prompt_value, lam, gain, cotangent, lengths):
    positions = jnp.arange(COMP_LEN, dtype=jnp.int32)
    key_places = jnp.arange(PROMPT + COMP_LEN, dtype=jnp.int32) - PROMPT
    visible = key_places[None, :] <= positions[:, None]

    def one_group(totals, inputs):
        queries, own_keys, own_values, grad_out, length = inputs
        all_keys = jnp.concatenate([prompt_key, own_keys], axis=0)
        all_values = jnp.concatenate([prompt_value, own_values], axis=0)
        live_rows = positions < length

        def one_head(head_inputs):
            head_query, head_keys, head_values, head_grad, weight_two, norm_gain = head_inputs
            return head_terms(head_query, head_keys, head_values, head_grad, weight_two, norm_gain, live_rows, visible)
        grad_q, grad_k, grad_v = lax.map(one_head, (jnp.transpose(queries, (1, 0, 2)), jnp.transpose(all_keys, (1, 0, 2)), jnp.transpose(all_values, (1, 0, 2)), jnp.transpose(grad_out, (1, 0, 2)), lam, gain))
        grad_q = jnp.transpose(grad_q, (1, 0, 2))
        grad_k = jnp.transpose(grad_k, (1, 0, 2))
        grad_v = jnp.transpose(grad_v, (1, 0, 2))
        totals = (totals[0] + grad_k[:PROMPT], totals[1] + grad_v[:PROMPT])
        return (totals, (grad_q.astype(jnp.bfloat16), grad_k[PROMPT:].astype(jnp.bfloat16), grad_v[PROMPT:].astype(jnp.bfloat16)))
    start_totals = (jnp.zeros((PROMPT, HEADS, 2 * HEAD), jnp.float32), jnp.zeros((PROMPT, HEADS, VDIM), jnp.float32))
    totals, stacked = lax.scan(one_group, start_totals, (comp_query, comp_key, comp_value, cotangent, lengths))
    return (stacked[0], stacked[1], stacked[2], totals[0].astype(jnp.bfloat16), totals[1].astype(jnp.bfloat16))
```

```python
import math

import jax
import jax.numpy as jnp
from jax import lax
from jax.experimental import pallas as pl
from jax.experimental.pallas import tpu as pltpu
from jax.sharding import PartitionSpec as P

F32, BF16 = jnp.float32, jnp.bfloat16
MESH = pl.DeviceIdType.MESH
SCALE = 128**-0.5
EXPO = SCALE * math.log2(math.e)
ROWS = 32
PROMPT_CHUNKS = ((0, 256, 0), (256, 256, 0))
COMP_CHUNKS = ((512, 256, 0), (768, 256, 256))
CHUNKS = PROMPT_CHUNKS + COMP_CHUNKS
SEQ_OFFSETS = ((1, 2), (0, 2), (1, 1), (1, 3), (0, 1), (0, 3), (1, 0))
COMP_OFFSETS = tuple((dy, dz) for dz in (4, 3, 5, 2, 6, 1, 7, 0) for dy in (1, 0) if (dy, dz) != (0, 0))


def nt(a, b):
    return lax.dot_general(a, b, (((1,), (1,)), ((), ())), preferred_element_type=F32)


def nn(a, b):
    return lax.dot_general(a, b, (((1,), (0,)), ((), ())), preferred_element_type=F32)


def iota(shape, dim):
    return lax.broadcasted_iota(jnp.int32, shape, dim)


def one_hot(hits):
    return jnp.where(hits, 1.0, 0.0).astype(BF16)


def half(i):
    return slice(i * 128, (i + 1) * 128)


def fold(x, op):
    return op(x.reshape(x.shape[0] // 8, 8, x.shape[1]), axis=0)


def merge(acc, part, first, op):
    if acc is None:
        return part
    if first:
        return jnp.concatenate([acc[:, :first], op(acc[:, first:], part)], axis=1)
    return op(acc, part)


def kernel(
    query_in, key_in, value_in, cot_in, pkey_in, pvalue_in, lam_in, gain_in, length_in,
    query_out, key_out, value_out, pkey_out, pvalue_out,
    qx, kx, vx, cx, pkx, pvx, lam, gain, length,
    prompt_send, kn, vn, qn, cn, kT, vT, cT,
    s1, s2, dm, mixT, ds1, ds2, dT,
    gq, gk, gv, gpack, part, sibling, zsend, zrecv, fsend, frecv, fout,
    in_sem, out_sem, ps_sem, pr_sem, fs_sem, fr_sem, cs_sem, cr_sem, zs_sem, zr_sem, as_sem, ar_sem,
):
    c, s = lax.axis_index("comp"), lax.axis_index("seq")
    core = lax.rem(c, 2)
    z = lax.rem(lax.div(c, 2), 8)
    y_hi = lax.div(c, 16)
    x = lax.rem(s, 4)
    y_lo = lax.div(s, 4)
    mate = (c + 1 - 2 * core, s)

    def seq_to(dy, dx):
        return lax.rem(y_lo + dy, 2) * 4 + lax.rem(x + dx, 4)

    def gather_to(dy, dx):
        comp = lax.rem(c + 16 * core, 32) if dy else c
        return comp, seq_to(dy, dx)

    def comp_at(dy, dz):
        return lax.rem(y_hi + dy, 2) * 8 + lax.rem(z + dz, 8)

    pairs = (
        (pkey_in, pkx), (pvalue_in, pvx), (query_in, qx), (key_in, kx), (value_in, vx), (cot_in, cx),
        (gain_in, gain), (lam_in, lam), (length_in, length),
    )
    loads = [pltpu.make_async_copy(src, dst, in_sem.at[i]) for i, (src, dst) in enumerate(pairs)]
    for load in loads:
        load.start()

    barrier = pltpu.get_barrier_semaphore()
    greet = [mate]
    greet += [gather_to(dy, dx) for dy, dx in SEQ_OFFSETS]
    greet += [(c, seq_to(dy, dx)) for dy, dx in SEQ_OFFSETS]
    greet += [(comp_at(dy, dz) * 2 + core, s) for dy, dz in COMP_OFFSETS]
    for peer in greet:
        pl.semaphore_signal(barrier, inc=1, device_id=peer, device_id_type=MESH)

    rows, cols = iota((256, 256), 0), iota((256, 256), 1)
    by_head = one_hot(cols == lax.rem(rows, 16) * 16 + lax.div(rows, 16))

    def repack(which, packed, keep):
        for b in range(4):
            got = nn(by_head, packed[b * 256 : (b + 1) * 256, :]).astype(BF16)
            for head in range(16):
                prompt_send[which, head // 2, head % 2, b * 16 : (b + 1) * 16, :] = got[head * 16 : (head + 1) * 16]
        for h in range(2):
            keep[h, pl.ds(pl.multiple_of(s * 64, 64), 64), :] = prompt_send[which, s, h]

    def prompt_copy(which, h, i, dy, dx):
        dst = (kn, vn)[which]
        here = pl.ds(pl.multiple_of(s * 64 + core * 32, 32), 32)
        return pltpu.make_async_remote_copy(
            prompt_send.at[which, seq_to(dy, dx), h, pl.ds(pl.multiple_of(core * 32, 32), 32)],
            dst.at[h, here],
            ps_sem.at[which, h, i],
            pr_sem.at[which, h, i],
            device_id=gather_to(dy, dx),
            device_id_type=MESH,
        )

    def forward_copy(which, h, i, dy, dx):
        dst = (kn, vn)[which]
        origin = lax.rem(y_lo + dy, 2) * 4 + lax.rem(x + 4 - dx, 4)
        there = pl.ds(pl.multiple_of(origin * 64 + core * 32, 32), 32)
        return pltpu.make_async_remote_copy(
            dst.at[h, there], dst.at[h, there], fs_sem.at[which, h, i], fr_sem.at[which, h, i],
            device_id=mate, device_id_type=MESH,
        )

    def prompt_start(which, h):
        for i, (dy, dx) in enumerate(SEQ_OFFSETS):
            prompt_copy(which, h, i, dy, dx).start()

    def prompt_forward(which, h):
        for i, (dy, dx) in reversed(tuple(enumerate(SEQ_OFFSETS))):
            prompt_copy(which, h, i, dy, dx).wait_recv()
            forward_copy(which, h, i, dy, dx).start()

    def prompt_arrived(which, h):
        for i, (dy, dx) in enumerate(SEQ_OFFSETS):
            forward_copy(which, h, i, dy, dx).wait_recv()

    loads[0].wait()
    repack(0, pkx, kn)
    pl.semaphore_wait(barrier, len(greet))
    prompt_start(0, 0)
    loads[1].wait()
    repack(1, pvx, vn)
    prompt_start(1, 0)
    prompt_start(0, 1)
    prompt_start(1, 1)

    apart = one_hot(cols == lax.rem(rows, 64) * 4 + lax.rem(lax.div(rows, 64), 2) * 2 + lax.div(rows, 128))
    together = one_hot(rows == lax.rem(cols, 64) * 4 + lax.rem(lax.div(cols, 64), 2) * 2 + lax.div(cols, 128))

    def unpack(first, second, first_to, second_to, first_row, second_row):
        for b in range(8):
            block = slice(b * 256, (b + 1) * 256)
            got = nn(apart, jnp.concatenate([first[block, :], second[block, :]], axis=1)).astype(BF16)
            for h in range(2):
                for i in range(2):
                    r = (h * 2 + i) * 64
                    t = b * 64
                    first_to[h, first_row + t : first_row + t + 64, half(i)] = got[r : r + 64, :128]
                    second_to[h, second_row + t : second_row + t + 64, half(i)] = got[r : r + 64, 128:]

    def turn(src, dst, h, first, last):
        for b in range(first, last, 256):
            dst[h, :, b : b + 256] = src[h, b : b + 256, :].T

    def scores(h, chunks, tops):
        for k0, n, q0 in chunks:
            for i, to in ((0, s1), (1, s2)):
                val = nt(kn[h, k0 : k0 + n, half(i)], qn[h, q0:, half(i)])
                for r in range(0, n, ROWS):
                    bit = val[r : r + ROWS]
                    if k0 >= 512:
                        seen = iota(bit.shape, 0) + (k0 - 512 + r) <= iota(bit.shape, 1) + q0
                        bit = jnp.where(seen, bit, -1e30)
                    to[h, k0 + r : k0 + r + ROWS, q0:] = bit
                    tops[i] = merge(tops[i], fold(bit, jnp.max), q0, jnp.maximum)

    def softmax(h, tops):
        sums = [None, None]
        for i, to in ((0, s1), (1, s2)):
            top = jnp.max(tops[i], axis=0, keepdims=True) * EXPO
            for k0, n, q0 in CHUNKS:
                for r in range(k0, k0 + n, ROWS):
                    e = jnp.exp2(to[h, r : r + ROWS, q0:] * EXPO - top[:, q0:])
                    to[h, r : r + ROWS, q0:] = e
                    sums[i] = merge(sums[i], fold(e, jnp.sum), q0, jnp.add)
        return [jnp.sum(total, axis=0, keepdims=True) for total in sums]

    def forward(h, sums):
        one, two = 1.0 / sums[0], lam[h] / sums[1]
        attn = None
        for k0, n, q0 in CHUNKS:
            for r in range(k0, k0 + n, ROWS):
                a1 = s1[h, r : r + ROWS, q0:] * one[:, q0:]
                a2 = s2[h, r : r + ROWS, q0:] * two[:, q0:]
                s1[h, r : r + ROWS, q0:] = a1
                s2[h, r : r + ROWS, q0:] = a2
                mixT[h, r : r + ROWS, q0:] = (a1 - a2).astype(BF16)
            attn = merge(attn, nn(vT[h, :, k0 : k0 + n], mixT[h, k0 : k0 + n, q0:]), q0, jnp.add)
        recip = lax.rsqrt(jnp.sum(attn * attn, axis=0, keepdims=True) * (1.0 / 256) + 1e-5)
        live = iota((1, 512), 1) < length[0]
        grad = jnp.where(live, cT[h].astype(F32), 0.0) * gains[:, h : h + 1]
        inner = jnp.sum(grad * attn, axis=0, keepdims=True) * (1.0 / 256)
        dT[h] = (recip * (grad - attn * (recip * recip * inner))).astype(BF16)

    def to_part(unit, k0, val, columns):
        for r in range(0, val.shape[0], 16):
            block = (k0 + r) // 16
            part[unit, block % 2, block // 2, :, columns] = val[r : r + 16].astype(BF16)

    def value_grads(h, chunks):
        for k0, n, q0 in chunks:
            val = nt(mixT[h, k0 : k0 + n, q0:], dT[h, :, q0:])
            if k0 < 512:
                to_part(2 * h, k0, val, slice(0, 256))
            else:
                gv[h, k0 - 512 : k0 - 512 + n, :] = val.astype(BF16)

    def key_grads(h, chunks):
        for k0, n, q0 in chunks:
            for i, ds in ((0, ds1), (1, ds2)):
                val = nn(ds[h, k0 : k0 + n, q0:], qn[h, q0:, half(i)]) * SCALE
                if k0 < 512:
                    to_part(2 * h + 1, k0, val, half(i))
                else:
                    gk[h, k0 - 512 : k0 - 512 + n, half(i)] = val.astype(BF16)

    def query_grads(h):
        for i, ds in ((0, ds1), (1, ds2)):
            total = None
            for k0, n, q0 in CHUNKS:
                total = merge(total, nn(kT[h, half(i), k0 : k0 + n], ds[h, k0 : k0 + n, q0:]), q0, jnp.add)
            gq[h, :, half(i)] = (total * SCALE).astype(BF16).T

    def row_sums(h):
        sums = [None, None]
        for k0, n, q0 in CHUNKS:
            val = nn(vn[h, k0 : k0 + n, :], dT[h, :, q0:])
            for r in range(0, n, ROWS):
                bit = val[r : r + ROWS]
                dm[k0 + r : k0 + r + ROWS, q0:] = bit
                for i, a in ((0, s1), (1, s2)):
                    prod = fold(a[h, k0 + r : k0 + r + ROWS, q0:] * bit, jnp.sum)
                    sums[i] = merge(sums[i], prod, q0, jnp.add)
        e1, e2 = [jnp.sum(total, axis=0, keepdims=True) for total in sums]
        return e1, e2 / lam[h]

    def score_grads(h, e1, e2, chunks):
        for k0, n, q0 in chunks:
            for r in range(k0, k0 + n, ROWS):
                bit = dm[r : r + ROWS, q0:]
                ds1[h, r : r + ROWS, q0:] = (s1[h, r : r + ROWS, q0:] * (bit - e1[:, q0:])).astype(BF16)
                ds2[h, r : r + ROWS, q0:] = (s2[h, r : r + ROWS, q0:] * (e2[:, q0:] - bit)).astype(BF16)

    def mate_copy(unit):
        return pltpu.make_async_remote_copy(
            part.at[unit, 1 - core], sibling.at[unit], cs_sem.at[unit], cr_sem.at[unit],
            device_id=mate, device_id_type=MESH,
        )

    def chip_copy(unit, i, dy, dz):
        return pltpu.make_async_remote_copy(
            zsend.at[unit, comp_at(dy, dz)], zrecv.at[unit, i], zs_sem.at[unit, i], zr_sem.at[unit, i],
            device_id=(comp_at(dy, dz) * 2 + core, s), device_id_type=MESH,
        )

    def send_chips(unit):
        mate_copy(unit).wait_recv()
        for b in range(16):
            zsend[unit, b] = (part[unit, core, b].astype(F32) + sibling[unit, b].astype(F32)).astype(BF16)
        for i, (dy, dz) in enumerate(COMP_OFFSETS):
            chip_copy(unit, i, dy, dz).start()

    def sum_chips(unit):
        total = zsend[unit, comp_at(0, 0)].astype(F32)
        for i, (dy, dz) in enumerate(COMP_OFFSETS):
            chip_copy(unit, i, dy, dz).wait_recv()
            total = total + zrecv[unit, i].astype(F32)
        return total

    loads[2].wait()
    loads[3].wait()
    unpack(qx, kx, qn, kn, 0, 512)
    tops = ([None, None], [None, None])
    scores(0, COMP_CHUNKS, tops[0])
    loads[4].wait()
    loads[5].wait()
    unpack(vx, cx, vn, cn, 512, 0)
    for load in loads[6:]:
        load.wait()
    gains = jnp.concatenate([gain[...], jnp.zeros((6, 256), F32)], axis=0).T
    for h in range(2):
        turn(cn, cT, h, 0, 512)
        turn(kn, kT, h, 512, 1024)
        turn(vn, vT, h, 512, 1024)
    scores(1, COMP_CHUNKS, tops[1])
    prompt_forward(0, 0)
    prompt_arrived(0, 0)
    scores(0, PROMPT_CHUNKS, tops[0])
    prompt_forward(1, 0)
    turn(kn, kT, 0, 0, 512)
    sums = softmax(0, tops[0])
    prompt_arrived(1, 0)
    turn(vn, vT, 0, 0, 512)
    prompt_forward(0, 1)
    forward(0, sums)
    value_grads(0, PROMPT_CHUNKS)
    mate_copy(0).start()
    prompt_forward(1, 1)
    e1, e2 = row_sums(0)
    send_chips(0)
    score_grads(0, e1, e2, PROMPT_CHUNKS)
    key_grads(0, PROMPT_CHUNKS)
    mate_copy(1).start()
    prompt_arrived(0, 1)
    scores(1, PROMPT_CHUNKS, tops[1])
    send_chips(1)
    score_grads(0, e1, e2, COMP_CHUNKS)
    sums = softmax(1, tops[1])
    prompt_arrived(1, 1)
    turn(vn, vT, 1, 0, 512)
    forward(1, sums)
    value_grads(1, PROMPT_CHUNKS)
    mate_copy(2).start()
    e1, e2 = row_sums(1)
    send_chips(2)
    score_grads(1, e1, e2, PROMPT_CHUNKS)
    key_grads(1, PROMPT_CHUNKS)
    mate_copy(3).start()
    score_grads(1, e1, e2, COMP_CHUNKS)
    turn(kn, kT, 1, 0, 512)
    send_chips(3)

    stores = []

    def hand_out(i, packed, out):
        for b in range(8):
            bits = [packed[h, b * 64 : (b + 1) * 64, half(i)] for h in range(2) for i in range(2)]
            gpack[i, b * 256 : (b + 1) * 256, :] = nn(together, jnp.concatenate(bits, axis=0)).astype(BF16)
        store = pltpu.make_async_copy(gpack.at[i], out, out_sem.at[i])
        store.start()
        stores.append(store)

    for h in range(2):
        value_grads(h, COMP_CHUNKS)
    hand_out(0, gv, value_out)
    for h in range(2):
        key_grads(h, COMP_CHUNKS)
    hand_out(1, gk, key_out)
    for h in range(2):
        query_grads(h)
    hand_out(2, gq, query_out)

    totals = [sum_chips(unit).astype(BF16) for unit in range(4)]
    done = jnp.concatenate([total[:, half(i)] for total in totals for i in range(2)], axis=0)
    rows, cols = iota((128, 128), 0), iota((128, 128), 1)
    to_owner = one_hot(cols == lax.rem(rows, 8) * 16 + lax.div(rows, 16) * 2 + lax.rem(lax.div(rows, 8), 2))
    routed = nn(to_owner, done).astype(BF16)
    for i in range(8):
        fsend[i] = routed[i * 16 : (i + 1) * 16]

    def owner_copy(i, dy, dx):
        return pltpu.make_async_remote_copy(
            fsend.at[seq_to(dy, dx)], frecv.at[s], as_sem.at[i], ar_sem.at[i],
            device_id=(c, seq_to(dy, dx)), device_id_type=MESH,
        )

    for i, (dy, dx) in enumerate(SEQ_OFFSETS):
        owner_copy(i, dy, dx).start()
    frecv[s] = fsend[s]
    place = lax.rem(lax.div(rows, 2), 8) * 16 + lax.rem(lax.div(rows, 16), 2) * 8 + lax.rem(rows, 2) * 4
    place = place + lax.div(rows, 64) * 2 + lax.rem(lax.div(rows, 32), 2)
    for i, (dy, dx) in enumerate(SEQ_OFFSETS):
        origin = lax.rem(y_lo + dy, 2) * 4 + lax.rem(x + 4 - dx, 4)
        pltpu.make_async_remote_copy(
            fsend.at[origin], frecv.at[origin], as_sem.at[i], ar_sem.at[i],
            device_id=(c, origin), device_id_type=MESH,
        ).wait_recv()
    owned = nn(one_hot(cols == place), frecv[...].reshape(128, 128)).astype(BF16)
    for i, out in ((0, pvalue_out), (1, pkey_out)):
        fout[i, :, :128] = owned[i * 64 : i * 64 + 32]
        fout[i, :, 128:] = owned[i * 64 + 32 : i * 64 + 64]
        store = pltpu.make_async_copy(fout.at[i], out, out_sem.at[3 + i])
        store.start()
        stores.append(store)

    for which in range(2):
        for h in range(2):
            for i, (dy, dx) in enumerate(SEQ_OFFSETS):
                prompt_copy(which, h, i, dy, dx).wait_send()
                forward_copy(which, h, i, dy, dx).wait_send()
    for unit in range(4):
        mate_copy(unit).wait_send()
        for i, (dy, dz) in enumerate(COMP_OFFSETS):
            chip_copy(unit, i, dy, dz).wait_send()
    for i, (dy, dx) in enumerate(SEQ_OFFSETS):
        owner_copy(i, dy, dx).wait_send()
    for store in stores:
        store.wait()


def interleaved(a):
    return a.reshape(512, 2, 2, 128).transpose(0, 2, 1, 3).reshape(2048, 128)


def by_token(a):
    return a.reshape(512, 2, 2, 128).transpose(0, 2, 1, 3).reshape(1, 512, 2, 256)


def shards(query, key, value, prompt_key, prompt_value, lam, gain, cotangent, lengths):
    vm = pltpu.VMEM
    dma = pltpu.SemaphoreType.DMA
    shape = jax.ShapeDtypeStruct
    anywhere = pl.BlockSpec(memory_space=pl.ANY)
    outs = pl.pallas_call(
        kernel,
        out_shape=[shape((2048, 128), BF16)] * 3 + [shape((32, 256), BF16)] * 2,
        in_specs=[anywhere] * 9,
        out_specs=[anywhere] * 5,
        scratch_shapes=[vm((2048, 128), BF16)] * 4
        + [vm((1024, 256), BF16)] * 2
        + [pltpu.SMEM((2,), F32), vm((2, 256), F32), pltpu.SMEM((1,), jnp.int32)]
        + [
            vm((2, 8, 2, 64, 256), BF16),
            vm((2, 1024, 256), BF16),
            vm((2, 1024, 256), BF16),
            vm((2, 512, 256), BF16),
            vm((2, 512, 256), BF16),
            vm((2, 256, 1024), BF16),
            vm((2, 256, 1024), BF16),
            vm((2, 256, 512), BF16),
            vm((2, 1024, 512), F32),
            vm((2, 1024, 512), F32),
            vm((1024, 512), F32),
            vm((2, 1024, 512), BF16),
            vm((2, 1024, 512), BF16),
            vm((2, 1024, 512), BF16),
            vm((2, 256, 512), BF16),
            vm((2, 512, 256), BF16),
            vm((2, 512, 256), BF16),
            vm((2, 512, 256), BF16),
            vm((3, 2048, 128), BF16),
            vm((4, 2, 16, 16, 256), BF16),
            vm((4, 16, 16, 256), BF16),
            vm((4, 16, 16, 256), BF16),
            vm((4, 15, 16, 256), BF16),
            vm((8, 16, 128), BF16),
            vm((8, 16, 128), BF16),
            vm((2, 32, 256), BF16),
        ]
        + [dma((9,)), dma((5,)), dma((2, 2, 7)), dma((2, 2, 7)), dma((2, 2, 7)), dma((2, 2, 7))]
        + [dma((4,)), dma((4,)), dma((4, 15)), dma((4, 15)), dma((7,)), dma((7,))],
        compiler_params=pltpu.CompilerParams(
            collective_id=0, has_side_effects=True, vmem_limit_bytes=48 * 2**20
        ),
    )(
        interleaved(query), interleaved(key), interleaved(value), interleaved(cotangent),
        prompt_key.reshape(1024, 256), prompt_value.reshape(1024, 256), lam, gain, lengths,
    )
    return (
        by_token(outs[0]), by_token(outs[1]), by_token(outs[2]),
        outs[3].reshape(2, 16, 256), outs[4].reshape(2, 16, 256),
    )


def solution(mesh):
    heads = P("comp", None, "seq", None)
    in_specs = (
        heads, heads, heads, P("seq", None, None), P("seq", None, None), P("seq"), P("seq", None), heads, P("comp"),
    )
    owners = P(("comp", "seq"), None, None)
    return jax.shard_map(
        shards, mesh=mesh, in_specs=in_specs, out_specs=(heads, heads, heads, owners, owners), check_vma=False
    )
```

```python
import math

import jax
import jax.numpy as jnp
from jax import lax
from jax.experimental import pallas as pl
from jax.experimental.pallas import tpu as pltpu
from jax.sharding import PartitionSpec as P

F32, BF16 = jnp.float32, jnp.bfloat16
MESH = pl.DeviceIdType.MESH
SCALE = 128**-0.5
EXPO = SCALE * math.log2(math.e)
ROWS = 32
PROMPT_CHUNKS = ((0, 256, 0), (256, 256, 0))
COMP_CHUNKS = ((512, 256, 0), (768, 256, 256))
CHUNKS = PROMPT_CHUNKS + COMP_CHUNKS
SEQ_OFFSETS = ((1, 2), (0, 2), (1, 1), (1, 3), (0, 1), (0, 3), (1, 0))
Z_OFFSETS = (4, 3, 5, 2, 6, 1, 7)
COMP_OFFSETS = tuple((dy, dz) for dz in (4, 3, 5, 2, 6, 1, 7, 0) for dy in (1, 0) if (dy, dz) != (0, 0))


def nt(a, b):
    return lax.dot_general(a, b, (((1,), (1,)), ((), ())), preferred_element_type=F32)


def nn(a, b):
    return lax.dot_general(a, b, (((1,), (0,)), ((), ())), preferred_element_type=F32)


def iota(shape, dim):
    return lax.broadcasted_iota(jnp.int32, shape, dim)


def one_hot(hits):
    return jnp.where(hits, 1.0, 0.0).astype(BF16)


def half(i):
    return slice(i * 128, (i + 1) * 128)


def fold(x, op):
    return op(x.reshape(x.shape[0] // 8, 8, x.shape[1]), axis=0)


def merge(acc, part, first, op):
    if acc is None:
        return part
    if first:
        return jnp.concatenate([acc[:, :first], op(acc[:, first:], part)], axis=1)
    return op(acc, part)


def kernel(
    query_in, key_in, value_in, cot_in, pkey_in, pvalue_in, lam_in, gain_in, length_in,
    query_out, key_out, value_out, pkey_out, pvalue_out,
    qx, kx, vx, cx, pkx, pvx, lam, gain, length,
    prompt_send, kn, vn, qn, cn, kT, vT, cT,
    s1, s2, dm, mixT, ds1, ds2, dT,
    gq, gk, gv, part, sibling, zsend, yrecv, zrecv, fsend, frecv,
    in_sem, ps_sem, pr_sem, fs_sem, fr_sem, cs_sem, cr_sem, ys_sem, yr_sem, zs_sem, zr_sem, as_sem, ar_sem,
):
    c, s = lax.axis_index("comp"), lax.axis_index("seq")
    core = lax.rem(c, 2)
    z = lax.rem(lax.div(c, 2), 8)
    y_hi = lax.div(c, 16)
    x = lax.rem(s, 4)
    y_lo = lax.div(s, 4)
    mate = (c + 1 - 2 * core, s)

    def seq_to(dy, dx):
        return lax.rem(y_lo + dy, 2) * 4 + lax.rem(x + dx, 4)

    def gather_to(dy, dx):
        comp = lax.rem(c + 16 * core, 32) if dy else c
        return comp, seq_to(dy, dx)

    def comp_at(dy, dz):
        return lax.rem(y_hi + dy, 2), lax.rem(z + dz, 8)

    def chip(dy, dz):
        other_y, other_z = comp_at(dy, dz)
        return (other_y * 8 + other_z) * 2 + core, s

    pairs = []
    for src, dst in ((pkey_in, pkx), (pvalue_in, pvx)):
        pairs += [(src.at[pl.ds(b * 256, 256)], dst.at[pl.ds(b * 256, 256)]) for b in range(4)]
    pairs += [(query_in, qx), (key_in, kx), (value_in, vx), (cot_in, cx), (gain_in, gain), (lam_in, lam), (length_in, length)]
    loads = [pltpu.make_async_copy(src, dst, in_sem.at[i]) for i, (src, dst) in enumerate(pairs)]
    for load in loads:
        load.start()

    barrier = pltpu.get_barrier_semaphore()
    greet = [mate]
    greet += [gather_to(dy, dx) for dy, dx in SEQ_OFFSETS]
    greet += [(c, seq_to(dy, dx)) for dy, dx in SEQ_OFFSETS]
    greet += [chip(dy, dz) for dy, dz in COMP_OFFSETS]
    for peer in greet:
        pl.semaphore_signal(barrier, inc=1, device_id=peer, device_id_type=MESH)

    rows, cols = iota((256, 256), 0), iota((256, 256), 1)
    by_head = one_hot(cols == lax.rem(rows, 16) * 16 + lax.div(rows, 16))

    def repack(which, packed, keep):
        for b in range(4):
            loads[which * 4 + b].wait()
            got = nn(by_head, packed[b * 256 : (b + 1) * 256, :]).astype(BF16)
            for head in range(16):
                prompt_send[which, head // 2, head % 2, b // 2, b % 2 * 16 : b % 2 * 16 + 16, :] = got[
                    head * 16 : (head + 1) * 16
                ]
        for h in range(2):
            keep[h, s, core] = prompt_send[which, s, h, core]

    def prompt_copy(which, h, dy, dx):
        return pltpu.make_async_remote_copy(
            prompt_send.at[which, seq_to(dy, dx), h, core],
            (kn, vn)[which].at[h, s, core],
            ps_sem.at[which, h],
            pr_sem.at[which, h],
            device_id=gather_to(dy, dx),
            device_id_type=MESH,
        )

    def prompt_all(which, h):
        bits = (kn, vn)[which].at[h, pl.ds(0, 7), core]
        return pltpu.make_async_remote_copy(
            bits, bits, ps_sem.at[which, h], pr_sem.at[which, h], device_id=mate, device_id_type=MESH
        )

    def forward_copy(which, h):
        bits = (kn, vn)[which].at[h, pl.ds(0, 8), core]
        return pltpu.make_async_remote_copy(
            bits, bits, fs_sem.at[which, h], fr_sem.at[which, h], device_id=mate, device_id_type=MESH
        )

    def prompt_start(which, h):
        for dy, dx in SEQ_OFFSETS:
            prompt_copy(which, h, dy, dx).start()

    def prompt_forward(which, h):
        prompt_all(which, h).wait_recv()
        forward_copy(which, h).start()

    def prompt_arrived(which, h):
        forward_copy(which, h).wait_recv()

    repack(0, pkx, kn)
    pl.semaphore_wait(barrier, len(greet))
    prompt_start(0, 0)
    repack(1, pvx, vn)
    prompt_start(1, 0)
    prompt_start(0, 1)
    prompt_start(1, 1)

    def rows_of(ref, h, first, count):
        return ref[h, first // 64 : (first + count) // 64].reshape(count, 256)

    apart = one_hot(cols == lax.rem(rows, 64) * 4 + lax.rem(lax.div(rows, 64), 2) * 2 + lax.div(rows, 128))
    together = one_hot(rows == lax.rem(cols, 64) * 4 + lax.rem(lax.div(cols, 64), 2) * 2 + lax.div(cols, 128))

    def unpack(first, second, first_to, second_to):
        for b in range(8):
            block = slice(b * 256, (b + 1) * 256)
            got = nn(apart, jnp.concatenate([first[block, :], second[block, :]], axis=1)).astype(BF16)
            for h in range(2):
                for i in range(2):
                    r = (h * 2 + i) * 64
                    t = b * 64
                    for to, val in ((first_to, got[r : r + 64, :128]), (second_to, got[r : r + 64, 128:])):
                        if to is kn or to is vn:
                            to[h, 8 + b, :, :, half(i)] = val.reshape(2, 32, 128)
                        else:
                            to[h, t : t + 64, half(i)] = val

    def turn(src, dst, h, first, last):
        for b in range(first, last, 256):
            rows = src[h, b : b + 256, :] if src is cn else rows_of(src, h, b, 256)
            dst[h, :, b : b + 256] = rows.T

    def scores(h, chunks, tops, sums):
        for k0, n, q0 in chunks:
            for i, to in ((0, s1), (1, s2)):
                keys = rows_of(kn, h, k0, n)[:, half(i)]
                some_tops, some_sums = [], []
                for q in range(q0, 512, 256):
                    val = nt(keys, qn[h, q : q + 256, half(i)])
                    if q == k0 - 512:
                        val = jnp.where(iota(val.shape, 0) <= iota(val.shape, 1), val, -1e30)
                    top = jnp.max(fold(val, jnp.max), axis=0, keepdims=True) * EXPO
                    e = jnp.exp2(val * EXPO - top)
                    to[h, k0 : k0 + n, q : q + 256] = e
                    some_tops.append(top)
                    some_sums.append(jnp.sum(fold(e, jnp.sum), axis=0, keepdims=True))
                tops[i][k0] = jnp.concatenate(some_tops, axis=1)
                sums[i][k0] = jnp.concatenate(some_sums, axis=1)

    def weights(h, tops, sums):
        found = []
        for i, factor in ((0, 1.0), (1, lam[h])):
            top, total = None, None
            for k0, _, q0 in CHUNKS:
                top = merge(top, tops[i][k0], q0, jnp.maximum)
            short = {k0: jnp.exp2(tops[i][k0] - top[:, q0:]) for k0, _, q0 in CHUNKS}
            for k0, _, q0 in CHUNKS:
                total = merge(total, sums[i][k0] * short[k0], q0, jnp.add)
            scale = factor / total
            found.append({k0: short[k0] * scale[:, q0:] for k0, _, q0 in CHUNKS})
        return found

    def forward(h, w):
        for k0, n, q0 in CHUNKS:
            for r in range(k0, k0 + n, ROWS):
                a1 = s1[h, r : r + ROWS, q0:] * w[0][k0]
                a2 = s2[h, r : r + ROWS, q0:] * w[1][k0]
                mixT[h, r : r + ROWS, q0:] = (a1 - a2).astype(BF16)
        for q in (0, 256):
            attn = nn(vT[h, :, : 768 + q], mixT[h, : 768 + q, q : q + 256])
            recip = lax.rsqrt(jnp.sum(attn * attn, axis=0, keepdims=True) * (1.0 / 256) + 1e-5)
            live = iota((1, 256), 1) + q < length[0]
            grad = jnp.where(live, cT[h, :, q : q + 256].astype(F32), 0.0) * gains[:, h : h + 1]
            inner = jnp.sum(grad * attn, axis=0, keepdims=True) * (1.0 / 256)
            dT[h, :, q : q + 256] = (recip * (grad - attn * (recip * recip * inner))).astype(BF16)

    def to_part(unit, k0, val, columns):
        for r in range(0, val.shape[0], 16):
            block = (k0 + r) // 16
            part[unit, block % 2, block // 2, :, columns] = val[r : r + 16].astype(BF16)

    def value_grads(h, chunks):
        for k0, n, q0 in chunks:
            val = nt(mixT[h, k0 : k0 + n, q0:], dT[h, :, q0:])
            if k0 < 512:
                to_part(2 * h, k0, val, slice(0, 256))
            else:
                gv[h, k0 - 512 : k0 - 512 + n, :] = val.astype(BF16)

    def key_grads(h, chunks):
        for k0, n, q0 in chunks:
            for i, ds in ((0, ds1), (1, ds2)):
                val = nn(ds[h, k0 : k0 + n, q0:], qn[h, q0:, half(i)]) * SCALE
                if k0 < 512:
                    to_part(2 * h + 1, k0, val, half(i))
                else:
                    gk[h, k0 - 512 : k0 - 512 + n, half(i)] = val.astype(BF16)

    def query_grads(h):
        for i, ds in ((0, ds1), (1, ds2)):
            for q in (0, 256):
                total = nn(kT[h, half(i), : 768 + q], ds[h, : 768 + q, q : q + 256])
                gq[h, q : q + 256, half(i)] = (total * SCALE).astype(BF16).T

    def row_sums(h, w):
        sums = [None, None]
        for k0, n, q0 in CHUNKS:
            val = nn(rows_of(vn, h, k0, n), dT[h, :, q0:])
            dm[k0 : k0 + n, q0:] = val
            for i, e in ((0, s1), (1, s2)):
                total = None
                for r in range(0, n, ROWS):
                    prod = fold(e[h, k0 + r : k0 + r + ROWS, q0:] * val[r : r + ROWS], jnp.sum)
                    total = prod if total is None else total + prod
                sums[i] = merge(sums[i], total * w[i][k0], q0, jnp.add)
        e1, e2 = [jnp.sum(total, axis=0, keepdims=True) for total in sums]
        return e1, e2 / lam[h]

    def score_grads(h, w, es, chunks):
        for k0, n, q0 in chunks:
            c1, c2 = [es[i][:, q0:] * w[i][k0] for i in range(2)]
            for r in range(k0, k0 + n, ROWS):
                bit = dm[r : r + ROWS, q0:]
                ds1[h, r : r + ROWS, q0:] = (s1[h, r : r + ROWS, q0:] * (bit * w[0][k0] - c1)).astype(BF16)
                ds2[h, r : r + ROWS, q0:] = (s2[h, r : r + ROWS, q0:] * (c2 - bit * w[1][k0])).astype(BF16)

    def mate_copy(unit):
        return pltpu.make_async_remote_copy(
            part.at[unit, 1 - core], sibling.at[unit], cs_sem.at[unit], cr_sem.at[unit],
            device_id=mate, device_id_type=MESH,
        )

    def y_copy(unit):
        return pltpu.make_async_remote_copy(
            zsend.at[unit, 1 - y_hi], yrecv.at[unit], ys_sem.at[unit], yr_sem.at[unit],
            device_id=chip(1, 0), device_id_type=MESH,
        )

    def chip_copy(unit, i, dy, dz):
        other_y, other_z = comp_at(dy, dz)
        return pltpu.make_async_remote_copy(
            zsend.at[unit, other_y, other_z], zrecv.at[unit, i], zs_sem.at[unit], zr_sem.at[unit],
            device_id=chip(dy, dz), device_id_type=MESH,
        )

    def chip_all(unit):
        bits = zrecv.at[unit, pl.ds(0, 7 if unit < 2 else 15)]
        return pltpu.make_async_remote_copy(
            bits, bits, zs_sem.at[unit], zr_sem.at[unit], device_id=mate, device_id_type=MESH
        )

    def add_mate(unit):
        mate_copy(unit).wait_recv()
        for y in range(2):
            for b in range(8):
                both = part[unit, core, y * 8 + b].astype(F32) + sibling[unit, y * 8 + b].astype(F32)
                zsend[unit, y, b] = both.astype(BF16)

    def send_y(unit):
        add_mate(unit)
        y_copy(unit).start()

    def send_z(unit):
        y_copy(unit).wait_recv()
        for b in range(8):
            both = zsend[unit, y_hi, b].astype(F32) + yrecv[unit, b].astype(F32)
            zsend[unit, y_hi, b] = both.astype(BF16)
        for i, dz in enumerate(Z_OFFSETS):
            chip_copy(unit, i, 0, dz).start()

    def send_direct(unit):
        add_mate(unit)
        for i, (dy, dz) in enumerate(COMP_OFFSETS):
            chip_copy(unit, i, dy, dz).start()

    def sum_chips(unit):
        chip_all(unit).wait_recv()
        total = zsend[unit, y_hi, z].astype(F32)
        for i in range(7 if unit < 2 else 15):
            total = total + zrecv[unit, i].astype(F32)
        return total

    loads[8].wait()
    loads[9].wait()
    unpack(qx, kx, qn, kn)
    tops, sums = ([{}, {}], [{}, {}]), ([{}, {}], [{}, {}])
    scores(0, COMP_CHUNKS, tops[0], sums[0])
    for load in loads[10:]:
        load.wait()
    unpack(vx, cx, vn, cn)
    gains = jnp.concatenate([gain[...], jnp.zeros((6, 256), F32)], axis=0).T
    scores(1, COMP_CHUNKS, tops[1], sums[1])
    for h in range(2):
        turn(cn, cT, h, 0, 512)
        turn(vn, vT, h, 512, 1024)
        turn(kn, kT, h, 512, 1024)
    prompt_forward(0, 0)
    prompt_arrived(0, 0)
    scores(0, PROMPT_CHUNKS, tops[0], sums[0])
    prompt_forward(1, 0)
    w0 = weights(0, tops[0], sums[0])
    prompt_arrived(1, 0)
    turn(vn, vT, 0, 0, 512)
    prompt_forward(0, 1)
    forward(0, w0)
    prompt_forward(1, 1)
    value_grads(0, PROMPT_CHUNKS)
    mate_copy(0).start()
    es0 = row_sums(0, w0)
    send_y(0)
    score_grads(0, w0, es0, PROMPT_CHUNKS)
    key_grads(0, PROMPT_CHUNKS)
    mate_copy(1).start()
    prompt_arrived(0, 1)
    scores(1, PROMPT_CHUNKS, tops[1], sums[1])
    score_grads(0, w0, es0, COMP_CHUNKS)
    send_y(1)
    w1 = weights(1, tops[1], sums[1])
    prompt_arrived(1, 1)
    turn(vn, vT, 1, 0, 512)
    forward(1, w1)
    send_z(0)
    value_grads(1, PROMPT_CHUNKS)
    mate_copy(2).start()
    es1 = row_sums(1, w1)
    send_z(1)
    send_direct(2)
    score_grads(1, w1, es1, PROMPT_CHUNKS)
    key_grads(1, PROMPT_CHUNKS)
    mate_copy(3).start()
    score_grads(1, w1, es1, COMP_CHUNKS)
    send_direct(3)

    def hand_out(packed, out):
        for b in range(8):
            bits = [packed[h, b * 64 : (b + 1) * 64, half(i)] for h in range(2) for i in range(2)]
            out[b * 256 : (b + 1) * 256, :] = nn(together, jnp.concatenate(bits, axis=0)).astype(BF16)

    for h in range(2):
        value_grads(h, COMP_CHUNKS)
    hand_out(gv, value_out)
    for h in range(2):
        key_grads(h, COMP_CHUNKS)
    hand_out(gk, key_out)
    for h in range(2):
        turn(kn, kT, h, 0, 512)
        query_grads(h)
    hand_out(gq, query_out)

    totals = [sum_chips(unit).astype(BF16) for unit in range(4)]
    done = jnp.concatenate([total[:, half(i)] for total in totals for i in range(2)], axis=0)
    rows, cols = iota((128, 128), 0), iota((128, 128), 1)
    to_owner = one_hot(cols == lax.rem(rows, 8) * 16 + lax.div(rows, 16) * 2 + lax.rem(lax.div(rows, 8), 2))
    routed = nn(to_owner, done).astype(BF16)
    for i in range(8):
        fsend[i] = routed[i * 16 : (i + 1) * 16]

    def owner_copy(dy, dx):
        return pltpu.make_async_remote_copy(
            fsend.at[seq_to(dy, dx)], frecv.at[s], as_sem.at[0], ar_sem.at[0],
            device_id=(c, seq_to(dy, dx)), device_id_type=MESH,
        )

    for dy, dx in SEQ_OFFSETS:
        owner_copy(dy, dx).start()
    frecv[s] = fsend[s]
    place = lax.rem(lax.div(rows, 2), 8) * 16 + lax.rem(lax.div(rows, 16), 2) * 8 + lax.rem(rows, 2) * 4
    place = place + lax.div(rows, 64) * 2 + lax.rem(lax.div(rows, 32), 2)
    bits = frecv.at[pl.ds(0, 7)]
    owner_all = pltpu.make_async_remote_copy(
        bits, bits, as_sem.at[0], ar_sem.at[0], device_id=mate, device_id_type=MESH
    )
    for which in range(2):
        for h in range(2):
            prompt_all(which, h).wait_send()
            forward_copy(which, h).wait_send()
    for unit in range(4):
        mate_copy(unit).wait_send()
        chip_all(unit).wait_send()
        if unit < 2:
            y_copy(unit).wait_send()
    owner_all.wait()
    owned = nn(one_hot(cols == place), frecv[...].reshape(128, 128)).astype(BF16)
    for i, out in ((0, pvalue_out), (1, pkey_out)):
        out[:, :128] = owned[i * 64 : i * 64 + 32]
        out[:, 128:] = owned[i * 64 + 32 : i * 64 + 64]


def writer(*refs):
    ins, outs, sem = refs[:5], refs[5:10], refs[10]
    stores = [pltpu.make_async_copy(src, dst, sem.at[i]) for i, (src, dst) in enumerate(zip(ins, outs))]
    for store in stores:
        store.start()
    for store in stores:
        store.wait()


def interleaved(a):
    return a.reshape(512, 2, 2, 128).transpose(0, 2, 1, 3).reshape(2048, 128)


def by_token(a):
    return a.reshape(512, 2, 2, 128).transpose(0, 2, 1, 3).reshape(1, 512, 2, 256)


def shards(query, key, value, prompt_key, prompt_value, lam, gain, cotangent, lengths):
    vm = pltpu.VMEM
    dma = pltpu.SemaphoreType.DMA
    shape = jax.ShapeDtypeStruct
    anywhere = pl.BlockSpec(memory_space=pltpu.HBM)
    results = [((2048, 128), BF16)] * 3 + [((32, 256), BF16)] * 2
    held = pl.pallas_call(
        kernel,
        out_shape=[vm(*result) for result in results],
        in_specs=[anywhere] * 9,
        out_specs=[pl.BlockSpec(memory_space=vm)] * 5,
        scratch_shapes=[vm((2048, 128), BF16)] * 4
        + [vm((1024, 256), BF16)] * 2
        + [pltpu.SMEM((2,), F32), vm((2, 256), F32), pltpu.SMEM((1,), jnp.int32)]
        + [
            vm((2, 8, 2, 2, 32, 256), BF16),
            vm((2, 16, 2, 32, 256), BF16),
            vm((2, 16, 2, 32, 256), BF16),
            vm((2, 512, 256), BF16),
            vm((2, 512, 256), BF16),
            vm((2, 256, 1024), BF16),
            vm((2, 256, 1024), BF16),
            vm((2, 256, 512), BF16),
            vm((2, 1024, 512), F32),
            vm((2, 1024, 512), F32),
            vm((1024, 512), F32),
            vm((2, 1024, 512), BF16),
            vm((2, 1024, 512), BF16),
            vm((2, 1024, 512), BF16),
            vm((2, 256, 512), BF16),
            vm((2, 512, 256), BF16),
            vm((2, 512, 256), BF16),
            vm((2, 512, 256), BF16),
            vm((4, 2, 16, 16, 256), BF16),
            vm((4, 16, 16, 256), BF16),
            vm((4, 2, 8, 16, 256), BF16),
            vm((2, 8, 16, 256), BF16),
            vm((4, 15, 16, 256), BF16),
            vm((8, 16, 128), BF16),
            vm((8, 16, 128), BF16),
        ]
        + [dma((15,)), dma((2, 2)), dma((2, 2)), dma((2, 2)), dma((2, 2))]
        + [dma((4,)), dma((4,)), dma((2,)), dma((2,)), dma((4,)), dma((4,)), dma((1,)), dma((1,))],
        compiler_params=pltpu.CompilerParams(
            collective_id=0, has_side_effects=True, vmem_limit_bytes=62 * 2**20
        ),
    )(
        interleaved(query), interleaved(key), interleaved(value), interleaved(cotangent),
        prompt_key.reshape(1024, 256), prompt_value.reshape(1024, 256), lam, gain, lengths,
    )
    outs = pl.pallas_call(
        writer,
        out_shape=[shape(*result) for result in results],
        in_specs=[anywhere] * 5,
        out_specs=[anywhere] * 5,
        scratch_shapes=[dma((5,))],
    )(*held)
    return (
        by_token(outs[0]), by_token(outs[1]), by_token(outs[2]),
        outs[3].reshape(2, 16, 256), outs[4].reshape(2, 16, 256),
    )


def solution(mesh):
    heads = P("comp", None, "seq", None)
    in_specs = (
        heads, heads, heads, P("seq", None, None), P("seq", None, None), P("seq"), P("seq", None), heads, P("comp"),
    )
    owners = P(("comp", "seq"), None, None)
    return jax.shard_map(
        shards, mesh=mesh, in_specs=in_specs, out_specs=(heads, heads, heads, owners, owners), check_vma=False
    )
```

```python
import math

import jax
import jax.numpy as jnp
from jax import lax
from jax.experimental import pallas as pl
from jax.experimental.pallas import tpu as pltpu
from jax.sharding import PartitionSpec as P

F32, BF16 = jnp.float32, jnp.bfloat16
MESH = pl.DeviceIdType.MESH
SCALE = 128**-0.5
EXPO = SCALE * math.log2(math.e)
ROWS = 32
PROMPT_CHUNKS = ((0, 256, 0), (256, 256, 0))
COMP_CHUNKS = ((512, 256, 0), (768, 256, 256))
CHUNKS = PROMPT_CHUNKS + COMP_CHUNKS
SEQ_OFFSETS = ((1, 2), (0, 2), (1, 1), (1, 3), (0, 1), (0, 3), (1, 0))
Z_OFFSETS = (4, 3, 5, 2, 6, 1, 7)
PLANE_OFFSETS = tuple(
    (dh, dy, dx) for dx in (2, 1, 3, 0) for dh, dy in ((1, 1), (1, 0), (0, 1), (0, 0)) if (dh, dy, dx) != (0, 0, 0)
)


def nt(a, b):
    return lax.dot_general(a, b, (((1,), (1,)), ((), ())), preferred_element_type=F32)


def nn(a, b):
    return lax.dot_general(a, b, (((1,), (0,)), ((), ())), preferred_element_type=F32)


def iota(shape, dim):
    return lax.broadcasted_iota(jnp.int32, shape, dim)


def one_hot(hits):
    return jnp.where(hits, 1.0, 0.0).astype(BF16)


def half(i):
    return slice(i * 128, (i + 1) * 128)


def fold(x, op):
    return op(x.reshape(x.shape[0] // 8, 8, x.shape[1]), axis=0)


def merge(acc, part, first, op):
    if acc is None:
        return part
    if first:
        return jnp.concatenate([acc[:, :first], op(acc[:, first:], part)], axis=1)
    return op(acc, part)


def kernel(
    query_in, key_in, value_in, cot_in, pkey_in, pvalue_in, lam_in, gain_in, length_in,
    query_out, key_out, value_out, pkey_out, pvalue_out,
    qx, kx, vx, cx, pkx, pvx, lam, gain, length,
    prompt_send, kn, vn, qn, cn, kT, vT, cT,
    s1, s2, dm, mixT, ds1, ds2, dT,
    gq, gk, gv, part, sibling, plane_send, plane_recv, z_send, z_recv,
    in_sem, ps_sem, pr_sem, fs_sem, fr_sem, cs_sem, cr_sem, ls_sem, lr_sem, zs_sem, zr_sem,
):
    c, s = lax.axis_index("comp"), lax.axis_index("seq")
    core = lax.rem(c, 2)
    z = lax.rem(lax.div(c, 2), 8)
    y_hi = lax.div(c, 16)
    x = lax.rem(s, 4)
    y_lo = lax.div(s, 4)
    mate = (c + 1 - 2 * core, s)

    def seq_to(dy, dx):
        return lax.rem(y_lo + dy, 2) * 4 + lax.rem(x + dx, 4)

    def gather_to(dy, dx):
        comp = lax.rem(c + 16 * core, 32) if dy else c
        return comp, seq_to(dy, dx)

    def plane_to(dh, dy, dx):
        return lax.rem(y_hi + dh, 2), seq_to(dy, dx)

    def on_plane(y, seq):
        return (y * 8 + z) * 2 + core, seq

    def on_z(other):
        return (y_hi * 8 + other) * 2 + core, s

    pairs = []
    for src, dst in ((pkey_in, pkx), (pvalue_in, pvx)):
        pairs += [(src.at[pl.ds(b * 256, 256)], dst.at[pl.ds(b * 256, 256)]) for b in range(4)]
    pairs += [(query_in, qx), (key_in, kx), (value_in, vx), (cot_in, cx), (gain_in, gain), (lam_in, lam), (length_in, length)]
    loads = [pltpu.make_async_copy(src, dst, in_sem.at[i]) for i, (src, dst) in enumerate(pairs)]
    for load in loads:
        load.start()

    barrier = pltpu.get_barrier_semaphore()
    greet = [mate]
    greet += [on_plane(*plane_to(*offsets)) for offsets in PLANE_OFFSETS]
    greet += [on_z(lax.rem(z + dz, 8)) for dz in Z_OFFSETS]
    for peer in greet:
        pl.semaphore_signal(barrier, inc=1, device_id=peer, device_id_type=MESH)

    rows, cols = iota((256, 256), 0), iota((256, 256), 1)
    by_head = one_hot(cols == lax.rem(rows, 16) * 16 + lax.div(rows, 16))

    def repack(which, packed, keep):
        for b in range(4):
            loads[which * 4 + b].wait()
            got = nn(by_head, packed[b * 256 : (b + 1) * 256, :]).astype(BF16)
            for head in range(16):
                prompt_send[which, head // 2, head % 2, b // 2, b % 2 * 16 : b % 2 * 16 + 16, :] = got[
                    head * 16 : (head + 1) * 16
                ]
        for h in range(2):
            keep[h, s, core] = prompt_send[which, s, h, core]

    def prompt_copy(which, h, dy, dx):
        return pltpu.make_async_remote_copy(
            prompt_send.at[which, seq_to(dy, dx), h, core],
            (kn, vn)[which].at[h, s, core],
            ps_sem.at[which, h],
            pr_sem.at[which, h],
            device_id=gather_to(dy, dx),
            device_id_type=MESH,
        )

    def prompt_all(which, h):
        bits = (kn, vn)[which].at[h, pl.ds(0, 7), core]
        return pltpu.make_async_remote_copy(
            bits, bits, ps_sem.at[which, h], pr_sem.at[which, h], device_id=mate, device_id_type=MESH
        )

    def forward_copy(which, h):
        bits = (kn, vn)[which].at[h, pl.ds(0, 8), core]
        return pltpu.make_async_remote_copy(
            bits, bits, fs_sem.at[which, h], fr_sem.at[which, h], device_id=mate, device_id_type=MESH
        )

    def prompt_start(which, h):
        for dy, dx in SEQ_OFFSETS:
            prompt_copy(which, h, dy, dx).start()

    def prompt_forward(which, h):
        prompt_all(which, h).wait_recv()
        forward_copy(which, h).start()

    def prompt_arrived(which, h):
        forward_copy(which, h).wait_recv()

    repack(0, pkx, kn)
    pl.semaphore_wait(barrier, len(greet))
    prompt_start(0, 0)
    repack(1, pvx, vn)
    prompt_start(1, 0)
    prompt_start(0, 1)
    prompt_start(1, 1)

    def rows_of(ref, h, first, count):
        return ref[h, first // 64 : (first + count) // 64].reshape(count, 256)

    apart = one_hot(cols == lax.rem(rows, 64) * 4 + lax.rem(lax.div(rows, 64), 2) * 2 + lax.div(rows, 128))
    together = one_hot(rows == lax.rem(cols, 64) * 4 + lax.rem(lax.div(cols, 64), 2) * 2 + lax.div(cols, 128))

    def unpack(first, second, first_to, second_to):
        for b in range(8):
            block = slice(b * 256, (b + 1) * 256)
            got = nn(apart, jnp.concatenate([first[block, :], second[block, :]], axis=1)).astype(BF16)
            for h in range(2):
                for i in range(2):
                    r = (h * 2 + i) * 64
                    t = b * 64
                    for to, val in ((first_to, got[r : r + 64, :128]), (second_to, got[r : r + 64, 128:])):
                        if to is kn or to is vn:
                            to[h, 8 + b, :, :, half(i)] = val.reshape(2, 32, 128)
                        else:
                            to[h, t : t + 64, half(i)] = val

    def turn(src, dst, h, first, last):
        for b in range(first, last, 256):
            rows = src[h, b : b + 256, :] if src is cn else rows_of(src, h, b, 256)
            dst[h, :, b : b + 256] = rows.T

    def scores(h, chunks, tops, sums):
        for k0, n, q0 in chunks:
            for i, to in ((0, s1), (1, s2)):
                keys = rows_of(kn, h, k0, n)[:, half(i)]
                some_tops, some_sums = [], []
                for q in range(q0, 512, 256):
                    val = nt(keys, qn[h, q : q + 256, half(i)])
                    if q == k0 - 512:
                        val = jnp.where(iota(val.shape, 0) <= iota(val.shape, 1), val, -1e30)
                    top = jnp.max(fold(val, jnp.max), axis=0, keepdims=True) * EXPO
                    e = jnp.exp2(val * EXPO - top)
                    to[h, k0 : k0 + n, q : q + 256] = e
                    some_tops.append(top)
                    some_sums.append(jnp.sum(fold(e, jnp.sum), axis=0, keepdims=True))
                tops[i][k0] = jnp.concatenate(some_tops, axis=1)
                sums[i][k0] = jnp.concatenate(some_sums, axis=1)

    def weights(h, tops, sums):
        found = []
        for i, factor in ((0, 1.0), (1, lam[h])):
            top, total = None, None
            for k0, _, q0 in CHUNKS:
                top = merge(top, tops[i][k0], q0, jnp.maximum)
            short = {k0: jnp.exp2(tops[i][k0] - top[:, q0:]) for k0, _, q0 in CHUNKS}
            for k0, _, q0 in CHUNKS:
                total = merge(total, sums[i][k0] * short[k0], q0, jnp.add)
            scale = factor / total
            found.append({k0: short[k0] * scale[:, q0:] for k0, _, q0 in CHUNKS})
        return found

    def forward(h, w):
        for k0, n, q0 in CHUNKS:
            for r in range(k0, k0 + n, ROWS):
                a1 = s1[h, r : r + ROWS, q0:] * w[0][k0]
                a2 = s2[h, r : r + ROWS, q0:] * w[1][k0]
                mixT[h, r : r + ROWS, q0:] = (a1 - a2).astype(BF16)
        for q in (0, 256):
            attn = nn(vT[h, :, : 768 + q], mixT[h, : 768 + q, q : q + 256])
            recip = lax.rsqrt(jnp.sum(attn * attn, axis=0, keepdims=True) * (1.0 / 256) + 1e-5)
            live = iota((1, 256), 1) + q < length[0]
            grad = jnp.where(live, cT[h, :, q : q + 256].astype(F32), 0.0) * gains[:, h : h + 1]
            inner = jnp.sum(grad * attn, axis=0, keepdims=True) * (1.0 / 256)
            dT[h, :, q : q + 256] = (recip * (grad - attn * (recip * recip * inner))).astype(BF16)

    def to_part(unit, k0, val, columns):
        for r in range(0, val.shape[0], 16):
            block = (k0 + r) // 16
            part[unit, block % 2, block // 2, :, columns] = val[r : r + 16].astype(BF16)

    def value_grads(h, chunks):
        for k0, n, q0 in chunks:
            val = nt(mixT[h, k0 : k0 + n, q0:], dT[h, :, q0:])
            if k0 < 512:
                to_part(2 * h, k0, val, slice(0, 256))
            else:
                gv[h, k0 - 512 : k0 - 512 + n, :] = val.astype(BF16)

    def key_grads(h, chunks):
        for k0, n, q0 in chunks:
            for i, ds in ((0, ds1), (1, ds2)):
                val = nn(ds[h, k0 : k0 + n, q0:], qn[h, q0:, half(i)]) * SCALE
                if k0 < 512:
                    to_part(2 * h + 1, k0, val, half(i))
                else:
                    gk[h, k0 - 512 : k0 - 512 + n, half(i)] = val.astype(BF16)

    def query_grads(h):
        for i, ds in ((0, ds1), (1, ds2)):
            for q in (0, 256):
                total = nn(kT[h, half(i), : 768 + q], ds[h, : 768 + q, q : q + 256])
                gq[h, q : q + 256, half(i)] = (total * SCALE).astype(BF16).T

    def row_sums(h, w):
        sums = [None, None]
        for k0, n, q0 in CHUNKS:
            val = nn(rows_of(vn, h, k0, n), dT[h, :, q0:])
            dm[k0 : k0 + n, q0:] = val
            for i, e in ((0, s1), (1, s2)):
                total = None
                for r in range(0, n, ROWS):
                    prod = fold(e[h, k0 + r : k0 + r + ROWS, q0:] * val[r : r + ROWS], jnp.sum)
                    total = prod if total is None else total + prod
                sums[i] = merge(sums[i], total * w[i][k0], q0, jnp.add)
        e1, e2 = [jnp.sum(total, axis=0, keepdims=True) for total in sums]
        return e1, e2 / lam[h]

    def score_grads(h, w, es, chunks):
        for k0, n, q0 in chunks:
            c1, c2 = [es[i][:, q0:] * w[i][k0] for i in range(2)]
            for r in range(k0, k0 + n, ROWS):
                bit = dm[r : r + ROWS, q0:]
                ds1[h, r : r + ROWS, q0:] = (s1[h, r : r + ROWS, q0:] * (bit * w[0][k0] - c1)).astype(BF16)
                ds2[h, r : r + ROWS, q0:] = (s2[h, r : r + ROWS, q0:] * (c2 - bit * w[1][k0])).astype(BF16)

    def mate_copy(unit):
        return pltpu.make_async_remote_copy(
            part.at[unit, 1 - core], sibling.at[unit], cs_sem.at[unit], cr_sem.at[unit],
            device_id=mate, device_id_type=MESH,
        )

    def plane_copy(unit, offsets):
        y, seq = plane_to(*offsets)
        return pltpu.make_async_remote_copy(
            plane_send.at[unit, y, seq], plane_recv.at[unit, y_hi, s], ls_sem.at[unit], lr_sem.at[unit],
            device_id=on_plane(y, seq), device_id_type=MESH,
        )

    def plane_all(unit):
        bits = z_recv.at[pl.ds(0, 15)]
        return pltpu.make_async_remote_copy(
            bits, bits, ls_sem.at[unit], lr_sem.at[unit], device_id=mate, device_id_type=MESH
        )

    def z_copy(unit, dz):
        other = lax.rem(z + dz, 8)
        return pltpu.make_async_remote_copy(
            z_send.at[unit, other], z_recv.at[unit * 8 + z], zs_sem.at[unit], zr_sem.at[unit],
            device_id=on_z(other), device_id_type=MESH,
        )

    def z_all(unit):
        bits = z_recv.at[pl.ds(unit * 8, 7)]
        return pltpu.make_async_remote_copy(
            bits, bits, zs_sem.at[unit], zr_sem.at[unit], device_id=mate, device_id_type=MESH
        )

    to_plane = one_hot(
        cols == lax.div(rows, 128) * 128 + lax.rem(lax.div(rows, 2), 8) * 16
        + lax.rem(lax.div(rows, 16), 8) * 2 + lax.rem(rows, 2)
    )
    to_z = to_plane[:128, :128]

    def send_plane(unit):
        mate_copy(unit).wait_recv()
        both = part[unit, core].reshape(256, 256).astype(F32) + sibling[unit].reshape(256, 256).astype(F32)
        plane_send[unit] = nn(to_plane, both.astype(BF16)).astype(BF16).reshape(2, 8, 16, 256)
        for offsets in PLANE_OFFSETS:
            plane_copy(unit, offsets).start()
        plane_recv[unit, y_hi, s] = plane_send[unit, y_hi, s]

    def send_z(unit):
        plane_all(unit).wait_recv()
        got = plane_recv[unit].reshape(2, 128, 256).astype(F32)
        z_send[unit] = nn(to_z, (got[0] + got[1]).astype(BF16)).astype(BF16).reshape(8, 16, 256)
        for dz in Z_OFFSETS:
            z_copy(unit, dz).start()
        z_recv[unit * 8 + z] = z_send[unit, z]

    def sum_z(unit):
        z_all(unit).wait_recv()
        total = z_recv[unit * 8].astype(F32)
        for i in range(1, 8):
            total = total + z_recv[unit * 8 + i].astype(F32)
        return total.astype(BF16)

    loads[8].wait()
    loads[9].wait()
    unpack(qx, kx, qn, kn)
    tops, sums = ([{}, {}], [{}, {}]), ([{}, {}], [{}, {}])
    scores(0, COMP_CHUNKS, tops[0], sums[0])
    for load in loads[10:]:
        load.wait()
    unpack(vx, cx, vn, cn)
    gains = jnp.concatenate([gain[...], jnp.zeros((6, 256), F32)], axis=0).T
    scores(1, COMP_CHUNKS, tops[1], sums[1])
    for h in range(2):
        turn(cn, cT, h, 0, 512)
        turn(vn, vT, h, 512, 1024)
        turn(kn, kT, h, 512, 1024)
    prompt_forward(0, 0)
    prompt_arrived(0, 0)
    scores(0, PROMPT_CHUNKS, tops[0], sums[0])
    prompt_forward(1, 0)
    w0 = weights(0, tops[0], sums[0])
    prompt_arrived(1, 0)
    turn(vn, vT, 0, 0, 512)
    prompt_forward(0, 1)
    forward(0, w0)
    prompt_forward(1, 1)
    value_grads(0, PROMPT_CHUNKS)
    mate_copy(0).start()
    es0 = row_sums(0, w0)
    send_plane(0)
    score_grads(0, w0, es0, PROMPT_CHUNKS)
    key_grads(0, PROMPT_CHUNKS)
    mate_copy(1).start()
    prompt_arrived(0, 1)
    scores(1, PROMPT_CHUNKS, tops[1], sums[1])
    score_grads(0, w0, es0, COMP_CHUNKS)
    send_plane(1)
    w1 = weights(1, tops[1], sums[1])
    prompt_arrived(1, 1)
    turn(vn, vT, 1, 0, 512)
    forward(1, w1)
    value_grads(1, PROMPT_CHUNKS)
    mate_copy(2).start()
    es1 = row_sums(1, w1)
    send_plane(2)
    score_grads(1, w1, es1, PROMPT_CHUNKS)
    key_grads(1, PROMPT_CHUNKS)
    mate_copy(3).start()
    score_grads(1, w1, es1, COMP_CHUNKS)
    send_plane(3)

    def hand_out(packed, out):
        for b in range(8):
            bits = [packed[h, b * 64 : (b + 1) * 64, half(i)] for h in range(2) for i in range(2)]
            out[b * 256 : (b + 1) * 256, :] = nn(together, jnp.concatenate(bits, axis=0)).astype(BF16)

    for h in range(2):
        value_grads(h, COMP_CHUNKS)
    for h in range(2):
        key_grads(h, COMP_CHUNKS)
    send_z(0)
    for h in range(2):
        turn(kn, kT, h, 0, 512)
        query_grads(h)
    send_z(1)
    hand_out(gv, value_out)
    send_z(2)
    hand_out(gk, key_out)
    send_z(3)
    hand_out(gq, query_out)

    for which in range(2):
        for h in range(2):
            prompt_all(which, h).wait_send()
            forward_copy(which, h).wait_send()
    for unit in range(4):
        mate_copy(unit).wait_send()
        plane_all(unit).wait_send()
    rows, cols = iota((32, 32), 0), iota((32, 32), 1)
    in_place = one_hot(cols == lax.rem(rows, 2) * 16 + lax.rem(lax.div(rows, 2), 8) * 2 + lax.div(rows, 16))
    for i, out in ((0, pvalue_out), (1, pkey_out)):
        out[...] = nn(in_place, jnp.concatenate([sum_z(i), sum_z(2 + i)], axis=0)).astype(BF16)
    for unit in range(4):
        z_all(unit).wait_send()


def writer(*refs):
    ins, outs, sem = refs[:5], refs[5:10], refs[10]
    stores = [pltpu.make_async_copy(src, dst, sem.at[i]) for i, (src, dst) in enumerate(zip(ins, outs))]
    for store in stores:
        store.start()
    for store in stores:
        store.wait()


def interleaved(a):
    return a.reshape(512, 2, 2, 128).transpose(0, 2, 1, 3).reshape(2048, 128)


def by_token(a):
    return a.reshape(512, 2, 2, 128).transpose(0, 2, 1, 3).reshape(1, 512, 2, 256)


def shards(query, key, value, prompt_key, prompt_value, lam, gain, cotangent, lengths):
    vm = pltpu.VMEM
    dma = pltpu.SemaphoreType.DMA
    shape = jax.ShapeDtypeStruct
    anywhere = pl.BlockSpec(memory_space=pltpu.HBM)
    results = [((2048, 128), BF16)] * 3 + [((32, 256), BF16)] * 2
    held = pl.pallas_call(
        kernel,
        out_shape=[vm(*result) for result in results],
        in_specs=[anywhere] * 9,
        out_specs=[pl.BlockSpec(memory_space=vm)] * 5,
        scratch_shapes=[vm((2048, 128), BF16)] * 4
        + [vm((1024, 256), BF16)] * 2
        + [pltpu.SMEM((2,), F32), vm((2, 256), F32), pltpu.SMEM((1,), jnp.int32)]
        + [
            vm((2, 8, 2, 2, 32, 256), BF16),
            vm((2, 16, 2, 32, 256), BF16),
            vm((2, 16, 2, 32, 256), BF16),
            vm((2, 512, 256), BF16),
            vm((2, 512, 256), BF16),
            vm((2, 256, 1024), BF16),
            vm((2, 256, 1024), BF16),
            vm((2, 256, 512), BF16),
            vm((2, 1024, 512), F32),
            vm((2, 1024, 512), F32),
            vm((1024, 512), F32),
            vm((2, 1024, 512), BF16),
            vm((2, 1024, 512), BF16),
            vm((2, 1024, 512), BF16),
            vm((2, 256, 512), BF16),
            vm((2, 512, 256), BF16),
            vm((2, 512, 256), BF16),
            vm((2, 512, 256), BF16),
            vm((4, 2, 16, 16, 256), BF16),
            vm((4, 16, 16, 256), BF16),
            vm((4, 2, 8, 16, 256), BF16),
            vm((4, 2, 8, 16, 256), BF16),
            vm((4, 8, 16, 256), BF16),
            vm((32, 16, 256), BF16),
        ]
        + [dma((15,)), dma((2, 2)), dma((2, 2)), dma((2, 2)), dma((2, 2))]
        + [dma((4,)), dma((4,)), dma((4,)), dma((4,)), dma((4,)), dma((4,))],
        compiler_params=pltpu.CompilerParams(
            collective_id=0, has_side_effects=True, vmem_limit_bytes=62 * 2**20
        ),
    )(
        interleaved(query), interleaved(key), interleaved(value), interleaved(cotangent),
        prompt_key.reshape(1024, 256), prompt_value.reshape(1024, 256), lam, gain, lengths,
    )
    outs = pl.pallas_call(
        writer,
        out_shape=[shape(*result) for result in results],
        in_specs=[pl.BlockSpec(memory_space=vm)] * 5,
        out_specs=[anywhere] * 5,
        scratch_shapes=[dma((5,))],
        compiler_params=pltpu.CompilerParams(vmem_limit_bytes=2 * 2**20),
    )(*held)
    return (
        by_token(outs[0]), by_token(outs[1]), by_token(outs[2]),
        outs[3].reshape(2, 16, 256), outs[4].reshape(2, 16, 256),
    )


def solution(mesh):
    heads = P("comp", None, "seq", None)
    in_specs = (
        heads, heads, heads, P("seq", None, None), P("seq", None, None), P("seq"), P("seq", None), heads, P("comp"),
    )
    owners = P(("comp", "seq"), None, None)
    return jax.shard_map(
        shards, mesh=mesh, in_specs=in_specs, out_specs=(heads, heads, heads, owners, owners), check_vma=False
    )
```

```python
import math

import jax
import jax.numpy as jnp
from jax import lax
from jax.experimental import pallas as pl
from jax.experimental.pallas import tpu as pltpu
from jax.sharding import PartitionSpec as P

F32, BF16 = jnp.float32, jnp.bfloat16
MESH = pl.DeviceIdType.MESH
SCALE = 128**-0.5
EXPO = SCALE * math.log2(math.e)
ROWS = 32
PROMPT_CHUNKS = ((0, 256, 0), (256, 256, 0))
COMP_CHUNKS = ((512, 256, 0), (768, 256, 256))
CHUNKS = PROMPT_CHUNKS + COMP_CHUNKS
SEQ_OFFSETS = ((1, 2), (0, 2), (1, 1), (1, 3), (0, 1), (0, 3), (1, 0))
Z_OFFSETS = (4, 3, 5, 2, 6, 1, 7)
PLANE_OFFSETS = tuple(
    (dh, dy, dx) for dx in (2, 1, 3, 0) for dh, dy in ((1, 1), (1, 0), (0, 1), (0, 0)) if (dh, dy, dx) != (0, 0, 0)
)

GROUPS = ((0, 1), (1, 1), (2, 1), (3, 1))


def nt(a, b):
    return lax.dot_general(a, b, (((1,), (1,)), ((), ())), preferred_element_type=F32)


def nn(a, b):
    return lax.dot_general(a, b, (((1,), (0,)), ((), ())), preferred_element_type=F32)


def iota(shape, dim):
    return lax.broadcasted_iota(jnp.int32, shape, dim)


def one_hot(hits):
    return jnp.where(hits, 1.0, 0.0).astype(BF16)


def half(i):
    return slice(i * 128, (i + 1) * 128)


def fold(x, op):
    return op(x.reshape(x.shape[0] // 8, 8, x.shape[1]), axis=0)


def merge(acc, part, first, op):
    if acc is None:
        return part
    if first:
        return jnp.concatenate([acc[:, :first], op(acc[:, first:], part)], axis=1)
    return op(acc, part)


def kernel(
    query_in, key_in, value_in, cot_in, pkey_in, pvalue_in, lam_in, gain_in, length_in,
    query_out, key_out, value_out, pkey_out, pvalue_out,
    qx, kx, vx, cx, pkx, pvx, lam, gain, length,
    prompt_send, kn, vn, qn, cn, kT, dn,
    s1, s2, dm, mixT, ds1, ds2, dA,
    gq, gk, gv, part, sibling, plane_send, plane_recv, z_send, z_recv,
    in_sem, ps_sem, pr_sem, fs_sem, fr_sem, cs_sem, cr_sem, ls_sem, lr_sem, zs_sem, zr_sem,
):
    c, s = lax.axis_index("comp"), lax.axis_index("seq")
    core = lax.rem(c, 2)
    z = lax.rem(lax.div(c, 2), 8)
    y_hi = lax.div(c, 16)
    x = lax.rem(s, 4)
    y_lo = lax.div(s, 4)
    mate = (c + 1 - 2 * core, s)

    def seq_to(dy, dx):
        return lax.rem(y_lo + dy, 2) * 4 + lax.rem(x + dx, 4)

    def gather_to(dy, dx):
        comp = lax.rem(c + 16 * core, 32) if dy else c
        return comp, seq_to(dy, dx)

    def plane_to(dh, dy, dx):
        return lax.rem(y_hi + dh, 2), seq_to(dy, dx)

    def on_plane(y, seq):
        return (y * 8 + z) * 2 + core, seq

    def on_z(other):
        return (y_hi * 8 + other) * 2 + core, s

    pairs = []
    for src, dst in ((pkey_in, pkx), (pvalue_in, pvx)):
        pairs += [(src.at[pl.ds(b * 256, 256)], dst.at[pl.ds(b * 256, 256)]) for b in range(4)]
    pairs += [(query_in, qx), (key_in, kx), (value_in, vx), (cot_in, cx), (gain_in, gain), (lam_in, lam), (length_in, length)]
    loads = [pltpu.make_async_copy(src, dst, in_sem.at[i]) for i, (src, dst) in enumerate(pairs)]

    barrier = pltpu.get_barrier_semaphore()
    greet = [mate]
    greet += [on_plane(*plane_to(*offsets)) for offsets in PLANE_OFFSETS]
    greet += [on_z(lax.rem(z + dz, 8)) for dz in Z_OFFSETS]
    for peer in greet:
        pl.semaphore_signal(barrier, inc=1, device_id=peer, device_id_type=MESH)

    for load in loads:
        load.start()

    rows, cols = iota((256, 256), 0), iota((256, 256), 1)
    by_head = one_hot(cols == lax.rem(rows, 16) * 16 + lax.div(rows, 16))

    def repack(which, packed, keep):
        for b in range(4):
            loads[which * 4 + b].wait()
            got = nn(by_head, packed[b * 256 : (b + 1) * 256, :]).astype(BF16)
            for head in range(16):
                prompt_send[which, head // 2, head % 2, b // 2, b % 2 * 16 : b % 2 * 16 + 16, :] = got[
                    head * 16 : (head + 1) * 16
                ]
        for h in range(2):
            keep[h, s, core] = prompt_send[which, s, h, core]

    def prompt_copy(which, h, dy, dx):
        return pltpu.make_async_remote_copy(
            prompt_send.at[which, seq_to(dy, dx), h, core],
            (kn, vn)[which].at[h, s, core],
            ps_sem.at[which, h],
            pr_sem.at[which, h],
            device_id=gather_to(dy, dx),
            device_id_type=MESH,
        )

    def prompt_all(which, h):
        bits = (kn, vn)[which].at[h, pl.ds(0, 7), core]
        return pltpu.make_async_remote_copy(
            bits, bits, ps_sem.at[which, h], pr_sem.at[which, h], device_id=mate, device_id_type=MESH
        )

    def forward_copy(which, h):
        bits = (kn, vn)[which].at[h, pl.ds(0, 8), core]
        return pltpu.make_async_remote_copy(
            bits, bits, fs_sem.at[which, h], fr_sem.at[which, h], device_id=mate, device_id_type=MESH
        )

    def prompt_start(which, h):
        for dy, dx in SEQ_OFFSETS:
            prompt_copy(which, h, dy, dx).start()

    def prompt_forward(which, h):
        prompt_all(which, h).wait_recv()
        forward_copy(which, h).start()

    def prompt_arrived(which, h):
        forward_copy(which, h).wait_recv()

    repack(0, pkx, kn)
    pl.semaphore_wait(barrier, len(greet))
    prompt_start(0, 0)
    repack(1, pvx, vn)
    prompt_start(1, 0)
    prompt_start(0, 1)
    prompt_start(1, 1)

    def rows_of(ref, h, first, count):
        return ref[h, first // 64 : (first + count) // 64].reshape(count, 256)

    apart = one_hot(cols == lax.rem(rows, 64) * 4 + lax.rem(lax.div(rows, 64), 2) * 2 + lax.div(rows, 128))
    together = one_hot(rows == lax.rem(cols, 64) * 4 + lax.rem(lax.div(cols, 64), 2) * 2 + lax.div(cols, 128))

    def unpack(first, second, first_to, second_to):
        for b in range(8):
            block = slice(b * 256, (b + 1) * 256)
            got = nn(apart, jnp.concatenate([first[block, :], second[block, :]], axis=1)).astype(BF16)
            for h in range(2):
                for i in range(2):
                    r = (h * 2 + i) * 64
                    t = b * 64
                    for to, val in ((first_to, got[r : r + 64, :128]), (second_to, got[r : r + 64, 128:])):
                        if to is kn or to is vn:
                            to[h, 8 + b, :, :, half(i)] = val.reshape(2, 32, 128)
                        else:
                            to[h, t : t + 64, half(i)] = val

    def turn(src, dst, h, first, last):
        for b in range(first, last, 256):
            dst[h, :, b : b + 256] = rows_of(src, h, b, 256).T

    def scores(h, chunks, tops, sums):
        for k0, n, q0 in chunks:
            for i, to in ((0, s1), (1, s2)):
                keys = rows_of(kn, h, k0, n)[:, half(i)]
                some_tops, some_sums = [], []
                for q in range(q0, 512, 256):
                    val = nt(keys, qn[h, q : q + 256, half(i)])
                    if q == k0 - 512:
                        val = jnp.where(iota(val.shape, 0) <= iota(val.shape, 1), val, -1e30)
                    top = jnp.max(fold(val, jnp.max), axis=0, keepdims=True) * EXPO
                    e = jnp.exp2(val * EXPO - top)
                    to[h, k0 : k0 + n, q : q + 256] = e
                    some_tops.append(top)
                    some_sums.append(jnp.sum(fold(e, jnp.sum), axis=0, keepdims=True))
                tops[i][k0] = jnp.concatenate(some_tops, axis=1)
                sums[i][k0] = jnp.concatenate(some_sums, axis=1)

    def weights(h, tops, sums):
        found = []
        for i, factor in ((0, 1.0), (1, lam[h])):
            top, total = None, None
            for k0, _, q0 in CHUNKS:
                top = merge(top, tops[i][k0], q0, jnp.maximum)
            short = {k0: jnp.exp2(tops[i][k0] - top[:, q0:]) for k0, _, q0 in CHUNKS}
            for k0, _, q0 in CHUNKS:
                total = merge(total, sums[i][k0] * short[k0], q0, jnp.add)
            scale = factor / total
            found.append({k0: short[k0] * scale[:, q0:] for k0, _, q0 in CHUNKS})
        return found

    def mix(h, w):
        for k0, n, q0 in CHUNKS:
            for r in range(k0, k0 + n, ROWS):
                a1 = s1[h, r : r + ROWS, q0:] * w[0][k0]
                a2 = s2[h, r : r + ROWS, q0:] * w[1][k0]
                mixT[h, r : r + ROWS, q0:] = (a1 - a2).astype(BF16)

    def tn(a, b):
        return lax.dot_general(a, b, (((0,), (0,)), ((), ())), preferred_element_type=F32)

    def wanted(h):
        live = iota((512, 1), 0) < length[0]
        dn[h] = jnp.where(live, cn[h].astype(F32), 0.0) * gain[h : h + 1, :]

    def forward(h):
        for q in (0, 256):
            attn = tn(mixT[h, : 768 + q, q : q + 256], rows_of(vn, h, 0, 768 + q))
            recip = lax.rsqrt(jnp.sum(attn * attn, axis=1, keepdims=True) * (1.0 / 256) + 1e-5)
            grad = dn[h, q : q + 256, :]
            inner = jnp.sum(grad * attn, axis=1, keepdims=True) * (1.0 / 256)
            dA[h, q : q + 256, :] = (recip * (grad - attn * (recip * recip * inner))).astype(BF16)

    def to_part(unit, k0, val, columns):
        for r in range(0, val.shape[0], 16):
            block = (k0 + r) // 16
            part[unit, block % 2, block // 2, :, columns] = val[r : r + 16].astype(BF16)

    def value_grads(h, chunks):
        for k0, n, q0 in chunks:
            val = nn(mixT[h, k0 : k0 + n, q0:], dA[h, q0:, :])
            if k0 < 512:
                to_part(2 * h, k0, val, slice(0, 256))
            else:
                gv[h, k0 - 512 : k0 - 512 + n, :] = val.astype(BF16)

    def key_grads(h, chunks):
        for k0, n, q0 in chunks:
            for i, ds in ((0, ds1), (1, ds2)):
                val = nn(ds[h, k0 : k0 + n, q0:], qn[h, q0:, half(i)]) * SCALE
                if k0 < 512:
                    to_part(2 * h + 1, k0, val, half(i))
                else:
                    gk[h, k0 - 512 : k0 - 512 + n, half(i)] = val.astype(BF16)

    def query_grads(h):
        for i, ds in ((0, ds1), (1, ds2)):
            for q in (0, 256):
                total = nn(kT[h, half(i), : 768 + q], ds[h, : 768 + q, q : q + 256])
                gq[h, q : q + 256, half(i)] = (total * SCALE).astype(BF16).T

    def row_sums(h, w):
        sums = [None, None]
        for k0, n, q0 in CHUNKS:
            val = nt(rows_of(vn, h, k0, n), dA[h, q0:, :])
            dm[h, k0 : k0 + n, q0:] = val
            for i, e in ((0, s1), (1, s2)):
                total = None
                for r in range(0, n, ROWS):
                    prod = fold(e[h, k0 + r : k0 + r + ROWS, q0:] * val[r : r + ROWS], jnp.sum)
                    total = prod if total is None else total + prod
                sums[i] = merge(sums[i], total * w[i][k0], q0, jnp.add)
        e1, e2 = [jnp.sum(total, axis=0, keepdims=True) for total in sums]
        return e1, e2 / lam[h]

    def score_grads(h, w, es, chunks):
        for k0, n, q0 in chunks:
            c1, c2 = [es[i][:, q0:] * w[i][k0] for i in range(2)]
            for r in range(k0, k0 + n, ROWS):
                bit = dm[h, r : r + ROWS, q0:]
                ds1[h, r : r + ROWS, q0:] = (s1[h, r : r + ROWS, q0:] * (bit * w[0][k0] - c1)).astype(BF16)
                ds2[h, r : r + ROWS, q0:] = (s2[h, r : r + ROWS, q0:] * (c2 - bit * w[1][k0])).astype(BF16)

    def mate_copy(first, count):
        units = pl.ds(first, count)
        return pltpu.make_async_remote_copy(
            part.at[units, 1 - core], sibling.at[units], cs_sem.at[first], cr_sem.at[first],
            device_id=mate, device_id_type=MESH,
        )

    def plane_copy(first, count, offsets):
        y, seq = plane_to(*offsets)
        units = pl.ds(first, count)
        return pltpu.make_async_remote_copy(
            plane_send.at[units, y, seq], plane_recv.at[units, y_hi, s], ls_sem.at[first], lr_sem.at[first],
            device_id=on_plane(y, seq), device_id_type=MESH,
        )

    def plane_all(first, count):
        bits = part.at[pl.ds(first, count), 0, pl.ds(0, 15)]
        return pltpu.make_async_remote_copy(
            bits, bits, ls_sem.at[first], lr_sem.at[first], device_id=mate, device_id_type=MESH
        )

    def z_copy(first, count, dz):
        other = lax.rem(z + dz, 8)
        units = pl.ds(first, count)
        return pltpu.make_async_remote_copy(
            z_send.at[units, other], z_recv.at[units, z], zs_sem.at[first], zr_sem.at[first],
            device_id=on_z(other), device_id_type=MESH,
        )

    def z_all(first, count):
        bits = z_recv.at[pl.ds(first, count), pl.ds(0, 7)]
        return pltpu.make_async_remote_copy(
            bits, bits, zs_sem.at[first], zr_sem.at[first], device_id=mate, device_id_type=MESH
        )

    to_plane = one_hot(
        cols == lax.div(rows, 128) * 128 + lax.rem(lax.div(rows, 2), 8) * 16
        + lax.rem(lax.div(rows, 16), 8) * 2 + lax.rem(rows, 2)
    )
    to_z = to_plane[:128, :128]

    def send_plane(first, count):
        mate_copy(first, count).wait_recv()
        for unit in range(first, first + count):
            both = part[unit, core].reshape(256, 256).astype(F32) + sibling[unit].reshape(256, 256).astype(F32)
            plane_send[unit] = nn(to_plane, both.astype(BF16)).astype(BF16).reshape(2, 8, 16, 256)
        for offsets in PLANE_OFFSETS:
            plane_copy(first, count, offsets).start()
        for unit in range(first, first + count):
            plane_recv[unit, y_hi, s] = plane_send[unit, y_hi, s]

    def send_z(first, count):
        plane_all(first, count).wait_recv()
        for unit in range(first, first + count):
            got = plane_recv[unit].reshape(2, 128, 256).astype(F32)
            z_send[unit] = nn(to_z, (got[0] + got[1]).astype(BF16)).astype(BF16).reshape(8, 16, 256)
        for dz in Z_OFFSETS:
            z_copy(first, count, dz).start()
        for unit in range(first, first + count):
            z_recv[unit, z] = z_send[unit, z]

    def sum_z(unit):
        return jnp.sum(z_recv[unit].astype(F32), axis=0).astype(BF16)

    loads[8].wait()
    loads[9].wait()
    unpack(qx, kx, qn, kn)
    tops, sums = ([{}, {}], [{}, {}]), ([{}, {}], [{}, {}])
    scores(0, COMP_CHUNKS, tops[0], sums[0])
    for load in loads[10:]:
        load.wait()
    unpack(vx, cx, vn, cn)
    scores(1, COMP_CHUNKS, tops[1], sums[1])
    for h in range(2):
        wanted(h)
        turn(kn, kT, h, 512, 1024)
    prompt_forward(0, 0)
    prompt_forward(1, 0)
    prompt_arrived(0, 0)
    scores(0, PROMPT_CHUNKS, tops[0], sums[0])
    w0 = weights(0, tops[0], sums[0])
    mix(0, w0)
    prompt_forward(0, 1)
    prompt_arrived(1, 0)
    forward(0)
    value_grads(0, PROMPT_CHUNKS)
    mate_copy(0, 1).start()
    prompt_forward(1, 1)
    es0 = row_sums(0, w0)
    score_grads(0, w0, es0, PROMPT_CHUNKS)
    key_grads(0, PROMPT_CHUNKS)
    mate_copy(1, 1).start()
    prompt_arrived(0, 1)
    scores(1, PROMPT_CHUNKS, tops[1], sums[1])
    w1 = weights(1, tops[1], sums[1])
    send_plane(0, 1)
    mix(1, w1)
    send_plane(1, 1)
    prompt_arrived(1, 1)
    forward(1)
    value_grads(1, PROMPT_CHUNKS)
    mate_copy(2, 1).start()
    es1 = row_sums(1, w1)
    score_grads(1, w1, es1, PROMPT_CHUNKS)
    key_grads(1, PROMPT_CHUNKS)
    mate_copy(3, 1).start()
    send_plane(2, 1)
    score_grads(1, w1, es1, COMP_CHUNKS)
    send_plane(3, 1)
    score_grads(0, w0, es0, COMP_CHUNKS)

    def hand_out(packed, out):
        for b in range(8):
            bits = [packed[h, b * 64 : (b + 1) * 64, half(i)] for h in range(2) for i in range(2)]
            out[b * 256 : (b + 1) * 256, :] = nn(together, jnp.concatenate(bits, axis=0)).astype(BF16)

    for h in range(2):
        value_grads(h, COMP_CHUNKS)
    for h in range(2):
        key_grads(h, COMP_CHUNKS)
    for h in range(2):
        turn(kn, kT, h, 0, 512)
        query_grads(h)
    send_z(0, 1)
    hand_out(gv, value_out)
    send_z(1, 1)
    hand_out(gk, key_out)
    hand_out(gq, query_out)
    send_z(2, 1)
    send_z(3, 1)

    for which in range(2):
        for h in range(2):
            prompt_all(which, h).wait_send()
            forward_copy(which, h).wait_send()
    for group in GROUPS:
        mate_copy(*group).wait_send()
        plane_all(*group).wait_send()
    rows, cols = iota((32, 32), 0), iota((32, 32), 1)
    in_place = one_hot(cols == lax.rem(rows, 2) * 16 + lax.rem(lax.div(rows, 2), 8) * 2 + lax.div(rows, 16))
    z_all(0, 1).wait()
    z_all(2, 1).wait()
    pvalue_out[...] = nn(in_place, jnp.concatenate([sum_z(0), sum_z(2)], axis=0)).astype(BF16)
    z_all(1, 1).wait()
    first_key = sum_z(1)
    z_all(3, 1).wait()
    pkey_out[...] = nn(in_place, jnp.concatenate([first_key, sum_z(3)], axis=0)).astype(BF16)


def writer(*refs):
    ins, outs, sem = refs[:5], refs[5:10], refs[10]
    stores = [pltpu.make_async_copy(src, dst, sem.at[i]) for i, (src, dst) in enumerate(zip(ins, outs))]
    for store in stores:
        store.start()
    for store in stores:
        store.wait()


def interleaved(a):
    return a.reshape(512, 2, 2, 128).transpose(0, 2, 1, 3).reshape(2048, 128)


def by_token(a):
    return a.reshape(512, 2, 2, 128).transpose(0, 2, 1, 3).reshape(1, 512, 2, 256)


def shards(query, key, value, prompt_key, prompt_value, lam, gain, cotangent, lengths):
    vm = pltpu.VMEM
    dma = pltpu.SemaphoreType.DMA
    shape = jax.ShapeDtypeStruct
    anywhere = pl.BlockSpec(memory_space=pltpu.HBM)
    results = [((2048, 128), BF16)] * 3 + [((32, 256), BF16)] * 2
    held = pl.pallas_call(
        kernel,
        out_shape=[vm(*result) for result in results],
        in_specs=[anywhere] * 9,
        out_specs=[pl.BlockSpec(memory_space=vm)] * 5,
        scratch_shapes=[vm((2048, 128), BF16)] * 4
        + [vm((1024, 256), BF16)] * 2
        + [pltpu.SMEM((2,), F32), vm((2, 256), F32), pltpu.SMEM((1,), jnp.int32)]
        + [
            vm((2, 8, 2, 2, 32, 256), BF16),
            vm((2, 16, 2, 32, 256), BF16),
            vm((2, 16, 2, 32, 256), BF16),
            vm((2, 512, 256), BF16),
            vm((2, 512, 256), BF16),
            vm((2, 256, 1024), BF16),
            vm((2, 512, 256), F32),
            vm((2, 1024, 512), F32),
            vm((2, 1024, 512), F32),
            vm((2, 1024, 512), F32),
            vm((2, 1024, 512), BF16),
            vm((2, 1024, 512), BF16),
            vm((2, 1024, 512), BF16),
            vm((2, 512, 256), BF16),
            vm((2, 512, 256), BF16),
            vm((2, 512, 256), BF16),
            vm((2, 512, 256), BF16),
            vm((4, 2, 16, 16, 256), BF16),
            vm((4, 16, 16, 256), BF16),
            vm((4, 2, 8, 16, 256), BF16),
            vm((4, 2, 8, 16, 256), BF16),
            vm((4, 8, 16, 256), BF16),
            vm((4, 8, 16, 256), BF16),
        ]
        + [dma((15,)), dma((2, 2)), dma((2, 2)), dma((2, 2)), dma((2, 2))]
        + [dma((4,)), dma((4,)), dma((4,)), dma((4,)), dma((4,)), dma((4,))],
        compiler_params=pltpu.CompilerParams(
            collective_id=0, has_side_effects=True, vmem_limit_bytes=62 * 2**20
        ),
    )(
        interleaved(query), interleaved(key), interleaved(value), interleaved(cotangent),
        prompt_key.reshape(1024, 256), prompt_value.reshape(1024, 256), lam, gain, lengths,
    )
    outs = pl.pallas_call(
        writer,
        out_shape=[shape(*result) for result in results],
        in_specs=[pl.BlockSpec(memory_space=vm)] * 5,
        out_specs=[anywhere] * 5,
        scratch_shapes=[dma((5,))],
        compiler_params=pltpu.CompilerParams(vmem_limit_bytes=2 * 2**20),
    )(*held)
    return (
        by_token(outs[0]), by_token(outs[1]), by_token(outs[2]),
        outs[3].reshape(2, 16, 256), outs[4].reshape(2, 16, 256),
    )


def solution(mesh):
    heads = P("comp", None, "seq", None)
    in_specs = (
        heads, heads, heads, P("seq", None, None), P("seq", None, None), P("seq"), P("seq", None), heads, P("comp"),
    )
    owners = P(("comp", "seq"), None, None)
    return jax.shard_map(
        shards, mesh=mesh, in_specs=in_specs, out_specs=(heads, heads, heads, owners, owners), check_vma=False
    )
```

```python
import math

import jax
import jax.numpy as jnp
from jax import lax
from jax.experimental import pallas as pl
from jax.experimental.pallas import tpu as pltpu
from jax.sharding import PartitionSpec as P

F32, BF16 = jnp.float32, jnp.bfloat16
MESH = pl.DeviceIdType.MESH
SCALE = 128**-0.5
EXPO = SCALE * math.log2(math.e)
ROWS = 32
PROMPT_CHUNKS = ((0, 256, 0), (256, 256, 0))
COMP_CHUNKS = ((512, 256, 0), (768, 256, 256))
CHUNKS = PROMPT_CHUNKS + COMP_CHUNKS
SEQ_OFFSETS = ((1, 2), (0, 2), (1, 1), (1, 3), (0, 1), (0, 3), (1, 0))
Z_OFFSETS = (4, 3, 5, 2, 6, 1, 7)
PLANE_OFFSETS = tuple(
    (dh, dy, dx) for dx in (2, 1, 3, 0) for dh, dy in ((1, 1), (1, 0), (0, 1), (0, 0)) if (dh, dy, dx) != (0, 0, 0)
)

GROUPS = ((0, 1), (1, 1), (2, 1), (3, 1))


def nt(a, b):
    return lax.dot_general(a, b, (((1,), (1,)), ((), ())), preferred_element_type=F32)


def nn(a, b):
    return lax.dot_general(a, b, (((1,), (0,)), ((), ())), preferred_element_type=F32)


def iota(shape, dim):
    return lax.broadcasted_iota(jnp.int32, shape, dim)


def one_hot(hits):
    return jnp.where(hits, 1.0, 0.0).astype(BF16)


def half(i):
    return slice(i * 128, (i + 1) * 128)


def fold(x, op):
    return op(x.reshape(x.shape[0] // 8, 8, x.shape[1]), axis=0)


def merge(acc, part, first, op):
    if acc is None:
        return part
    if first:
        return jnp.concatenate([acc[:, :first], op(acc[:, first:], part)], axis=1)
    return op(acc, part)


def kernel(
    query_in, key_in, value_in, cot_in, pkey_in, pvalue_in, lam_in, gain_in, length_in,
    query_out, key_out, value_out, pkey_out, pvalue_out,
    qx, kx, vx, cx, pkx, pvx, lam, gain, length,
    prompt_send, kn, vn, qn, cn, kT, dn,
    s1, s2, dm, mixT, ds1, ds2, dA,
    gq, gk, gv, part, sibling, plane_send, plane_recv, z_send, z_recv,
    in_sem, ps_sem, pr_sem, fs_sem, fr_sem, cs_sem, cr_sem, ls_sem, lr_sem, zs_sem, zr_sem,
):
    c, s = lax.axis_index("comp"), lax.axis_index("seq")
    core = lax.rem(c, 2)
    z = lax.rem(lax.div(c, 2), 8)
    y_hi = lax.div(c, 16)
    x = lax.rem(s, 4)
    y_lo = lax.div(s, 4)
    mate = (c + 1 - 2 * core, s)

    def seq_to(dy, dx):
        return lax.rem(y_lo + dy, 2) * 4 + lax.rem(x + dx, 4)

    def gather_to(dy, dx):
        comp = lax.rem(c + 16 * core, 32) if dy else c
        return comp, seq_to(dy, dx)

    def plane_to(dh, dy, dx):
        return lax.rem(y_hi + dh, 2), seq_to(dy, dx)

    def on_plane(y, seq):
        return (y * 8 + z) * 2 + core, seq

    def on_z(other):
        return (y_hi * 8 + other) * 2 + core, s

    pairs = []
    for src, dst in ((pkey_in, pkx), (pvalue_in, pvx)):
        pairs += [(src.at[pl.ds(b * 256, 256)], dst.at[pl.ds(b * 256, 256)]) for b in range(4)]
    pairs += [(query_in, qx), (key_in, kx), (value_in, vx), (cot_in, cx), (gain_in, gain), (lam_in, lam), (length_in, length)]
    loads = [pltpu.make_async_copy(src, dst, in_sem.at[i]) for i, (src, dst) in enumerate(pairs)]

    barrier = pltpu.get_barrier_semaphore()
    greet = [mate]
    greet += [on_plane(*plane_to(*offsets)) for offsets in PLANE_OFFSETS]
    greet += [on_z(lax.rem(z + dz, 8)) for dz in Z_OFFSETS]
    for peer in greet:
        pl.semaphore_signal(barrier, inc=1, device_id=peer, device_id_type=MESH)

    for load in loads:
        load.start()

    rows, cols = iota((256, 256), 0), iota((256, 256), 1)
    by_head = one_hot(cols == lax.rem(rows, 16) * 16 + lax.div(rows, 16))

    def repack(which, packed, keep):
        for b in range(4):
            loads[which * 4 + b].wait()
            got = nn(by_head, packed[b * 256 : (b + 1) * 256, :]).astype(BF16)
            for head in range(16):
                prompt_send[which, head // 2, head % 2, b // 2, b % 2 * 16 : b % 2 * 16 + 16, :] = got[
                    head * 16 : (head + 1) * 16
                ]
        for h in range(2):
            keep[h, s, core] = prompt_send[which, s, h, core]

    def prompt_copy(which, h, dy, dx):
        return pltpu.make_async_remote_copy(
            prompt_send.at[which, seq_to(dy, dx), h, core],
            (kn, vn)[which].at[h, s, core],
            ps_sem.at[which, h],
            pr_sem.at[which, h],
            device_id=gather_to(dy, dx),
            device_id_type=MESH,
        )

    def prompt_all(which, h):
        bits = (kn, vn)[which].at[h, pl.ds(0, 7), core]
        return pltpu.make_async_remote_copy(
            bits, bits, ps_sem.at[which, h], pr_sem.at[which, h], device_id=mate, device_id_type=MESH
        )

    def forward_copy(which, h):
        bits = (kn, vn)[which].at[h, pl.ds(0, 8), core]
        return pltpu.make_async_remote_copy(
            bits, bits, fs_sem.at[which, h], fr_sem.at[which, h], device_id=mate, device_id_type=MESH
        )

    def prompt_start(which, h):
        for dy, dx in SEQ_OFFSETS:
            prompt_copy(which, h, dy, dx).start()

    def prompt_forward(which, h):
        prompt_all(which, h).wait_recv()
        forward_copy(which, h).start()

    def prompt_arrived(which, h):
        forward_copy(which, h).wait_recv()

    repack(0, pkx, kn)
    pl.semaphore_wait(barrier, len(greet))
    prompt_start(0, 0)
    repack(1, pvx, vn)
    prompt_start(1, 0)

    def rows_of(ref, h, first, count):
        return ref[h, first // 64 : (first + count) // 64].reshape(count, 256)

    apart = one_hot(cols == lax.rem(rows, 64) * 4 + lax.rem(lax.div(rows, 64), 2) * 2 + lax.div(rows, 128))
    together = one_hot(rows == lax.rem(cols, 64) * 4 + lax.rem(lax.div(cols, 64), 2) * 2 + lax.div(cols, 128))

    def unpack(first, second, first_to, second_to):
        for b in range(8):
            block = slice(b * 256, (b + 1) * 256)
            got = nn(apart, jnp.concatenate([first[block, :], second[block, :]], axis=1)).astype(BF16)
            for h in range(2):
                for i in range(2):
                    r = (h * 2 + i) * 64
                    t = b * 64
                    for to, val in ((first_to, got[r : r + 64, :128]), (second_to, got[r : r + 64, 128:])):
                        if to is kn or to is vn:
                            to[h, 8 + b, :, :, half(i)] = val.reshape(2, 32, 128)
                        else:
                            to[h, t : t + 64, half(i)] = val

    def turn(src, dst, h, first, last):
        for b in range(first, last, 256):
            dst[h, :, b : b + 256] = rows_of(src, h, b, 256).T

    def scores(h, chunks, tops, sums):
        for k0, n, q0 in chunks:
            for i, to in ((0, s1), (1, s2)):
                keys = rows_of(kn, h, k0, n)[:, half(i)]
                some_tops, some_sums = [], []
                for q in range(q0, 512, 256):
                    val = nt(keys, qn[h, q : q + 256, half(i)])
                    if q == k0 - 512:
                        val = jnp.where(iota(val.shape, 0) <= iota(val.shape, 1), val, -1e30)
                    top = jnp.max(fold(val, jnp.max), axis=0, keepdims=True) * EXPO
                    e = jnp.exp2(val * EXPO - top)
                    to[h, k0 : k0 + n, q : q + 256] = e
                    some_tops.append(top)
                    some_sums.append(jnp.sum(fold(e, jnp.sum), axis=0, keepdims=True))
                tops[i][k0] = jnp.concatenate(some_tops, axis=1)
                sums[i][k0] = jnp.concatenate(some_sums, axis=1)

    def weights(h, tops, sums):
        found = []
        for i, factor in ((0, 1.0), (1, lam[h])):
            top, total = None, None
            for k0, _, q0 in CHUNKS:
                top = merge(top, tops[i][k0], q0, jnp.maximum)
            short = {k0: jnp.exp2(tops[i][k0] - top[:, q0:]) for k0, _, q0 in CHUNKS}
            for k0, _, q0 in CHUNKS:
                total = merge(total, sums[i][k0] * short[k0], q0, jnp.add)
            scale = factor / total
            found.append({k0: short[k0] * scale[:, q0:] for k0, _, q0 in CHUNKS})
        return found

    def mix(h, w):
        for k0, n, q0 in CHUNKS:
            for r in range(k0, k0 + n, ROWS):
                a1 = s1[h, r : r + ROWS, q0:] * w[0][k0]
                a2 = s2[h, r : r + ROWS, q0:] * w[1][k0]
                mixT[h, r : r + ROWS, q0:] = (a1 - a2).astype(BF16)

    def tn(a, b):
        return lax.dot_general(a, b, (((0,), (0,)), ((), ())), preferred_element_type=F32)

    def wanted(h):
        live = iota((512, 1), 0) < length[0]
        dn[h] = jnp.where(live, cn[h].astype(F32), 0.0) * gain[h : h + 1, :]

    def forward(h):
        for q in (0, 256):
            attn = tn(mixT[h, : 768 + q, q : q + 256], rows_of(vn, h, 0, 768 + q))
            recip = lax.rsqrt(jnp.sum(attn * attn, axis=1, keepdims=True) * (1.0 / 256) + 1e-5)
            grad = dn[h, q : q + 256, :]
            inner = jnp.sum(grad * attn, axis=1, keepdims=True) * (1.0 / 256)
            dA[h, q : q + 256, :] = (recip * (grad - attn * (recip * recip * inner))).astype(BF16)

    def to_part(unit, k0, val, columns):
        for r in range(0, val.shape[0], 16):
            block = (k0 + r) // 16
            part[unit, block % 2, block // 2, :, columns] = val[r : r + 16].astype(BF16)

    def value_grads(h, chunks):
        for k0, n, q0 in chunks:
            val = nn(mixT[h, k0 : k0 + n, q0:], dA[h, q0:, :])
            if k0 < 512:
                to_part(2 * h, k0, val, slice(0, 256))
            else:
                gv[h, k0 - 512 : k0 - 512 + n, :] = val.astype(BF16)

    def key_grads(h, chunks):
        for k0, n, q0 in chunks:
            for i, ds in ((0, ds1), (1, ds2)):
                val = nn(ds[h, k0 : k0 + n, q0:], qn[h, q0:, half(i)]) * SCALE
                if k0 < 512:
                    to_part(2 * h + 1, k0, val, half(i))
                else:
                    gk[h, k0 - 512 : k0 - 512 + n, half(i)] = val.astype(BF16)

    def query_grads(h):
        for i, ds in ((0, ds1), (1, ds2)):
            for q in (0, 256):
                total = nn(kT[h, half(i), : 768 + q], ds[h, : 768 + q, q : q + 256])
                gq[h, q : q + 256, half(i)] = (total * SCALE).astype(BF16).T

    def row_sums(h, w):
        sums = [None, None]
        for k0, n, q0 in CHUNKS:
            val = nt(rows_of(vn, h, k0, n), dA[h, q0:, :])
            dm[h, k0 : k0 + n, q0:] = val
            for i, e in ((0, s1), (1, s2)):
                total = None
                for r in range(0, n, ROWS):
                    prod = fold(e[h, k0 + r : k0 + r + ROWS, q0:] * val[r : r + ROWS], jnp.sum)
                    total = prod if total is None else total + prod
                sums[i] = merge(sums[i], total * w[i][k0], q0, jnp.add)
        e1, e2 = [jnp.sum(total, axis=0, keepdims=True) for total in sums]
        return e1, e2 / lam[h]

    def score_grads(h, w, es, chunks):
        for k0, n, q0 in chunks:
            c1, c2 = [es[i][:, q0:] * w[i][k0] for i in range(2)]
            for r in range(k0, k0 + n, ROWS):
                bit = dm[h, r : r + ROWS, q0:]
                ds1[h, r : r + ROWS, q0:] = (s1[h, r : r + ROWS, q0:] * (bit * w[0][k0] - c1)).astype(BF16)
                ds2[h, r : r + ROWS, q0:] = (s2[h, r : r + ROWS, q0:] * (c2 - bit * w[1][k0])).astype(BF16)

    def mate_copy(first, count):
        units = pl.ds(first, count)
        return pltpu.make_async_remote_copy(
            part.at[units, 1 - core], sibling.at[units], cs_sem.at[first], cr_sem.at[first],
            device_id=mate, device_id_type=MESH,
        )

    def plane_copy(first, count, offsets):
        y, seq = plane_to(*offsets)
        units = pl.ds(first, count)
        return pltpu.make_async_remote_copy(
            plane_send.at[units, y, seq], plane_recv.at[units, y_hi, s], ls_sem.at[first], lr_sem.at[first],
            device_id=on_plane(y, seq), device_id_type=MESH,
        )

    def plane_all(first, count):
        bits = part.at[pl.ds(first, count), 0, pl.ds(0, 15)]
        return pltpu.make_async_remote_copy(
            bits, bits, ls_sem.at[first], lr_sem.at[first], device_id=mate, device_id_type=MESH
        )

    def z_copy(first, count, dz):
        other = lax.rem(z + dz, 8)
        units = pl.ds(first, count)
        return pltpu.make_async_remote_copy(
            z_send.at[units, other], z_recv.at[units, z], zs_sem.at[first], zr_sem.at[first],
            device_id=on_z(other), device_id_type=MESH,
        )

    def z_all(first, count):
        bits = z_recv.at[pl.ds(first, count), pl.ds(0, 7)]
        return pltpu.make_async_remote_copy(
            bits, bits, zs_sem.at[first], zr_sem.at[first], device_id=mate, device_id_type=MESH
        )

    to_plane = one_hot(
        cols == lax.div(rows, 128) * 128 + lax.rem(lax.div(rows, 2), 8) * 16
        + lax.rem(lax.div(rows, 16), 8) * 2 + lax.rem(rows, 2)
    )
    to_z = to_plane[:128, :128]

    def send_plane(first, count):
        mate_copy(first, count).wait_recv()
        for unit in range(first, first + count):
            both = part[unit, core].reshape(256, 256).astype(F32) + sibling[unit].reshape(256, 256).astype(F32)
            plane_send[unit] = nn(to_plane, both.astype(BF16)).astype(BF16).reshape(2, 8, 16, 256)
        for offsets in PLANE_OFFSETS:
            plane_copy(first, count, offsets).start()
        for unit in range(first, first + count):
            plane_recv[unit, y_hi, s] = plane_send[unit, y_hi, s]

    def send_z(first, count):
        plane_all(first, count).wait_recv()
        for unit in range(first, first + count):
            got = plane_recv[unit].reshape(2, 128, 256).astype(F32)
            z_send[unit] = nn(to_z, (got[0] + got[1]).astype(BF16)).astype(BF16).reshape(8, 16, 256)
        for dz in Z_OFFSETS:
            z_copy(first, count, dz).start()
        for unit in range(first, first + count):
            z_recv[unit, z] = z_send[unit, z]

    def sum_z(unit):
        return jnp.sum(z_recv[unit].astype(F32), axis=0).astype(BF16)

    loads[8].wait()
    loads[9].wait()
    unpack(qx, kx, qn, kn)
    prompt_start(0, 1)
    prompt_start(1, 1)
    tops, sums = ([{}, {}], [{}, {}]), ([{}, {}], [{}, {}])
    scores(0, COMP_CHUNKS, tops[0], sums[0])
    for load in loads[10:]:
        load.wait()
    unpack(vx, cx, vn, cn)
    scores(1, COMP_CHUNKS, tops[1], sums[1])
    for h in range(2):
        wanted(h)
        turn(kn, kT, h, 512, 1024)
    prompt_forward(0, 0)
    prompt_forward(1, 0)
    prompt_arrived(0, 0)
    scores(0, PROMPT_CHUNKS, tops[0], sums[0])
    w0 = weights(0, tops[0], sums[0])
    mix(0, w0)
    prompt_forward(0, 1)
    prompt_arrived(1, 0)
    forward(0)
    value_grads(0, PROMPT_CHUNKS)
    mate_copy(0, 1).start()
    prompt_forward(1, 1)
    es0 = row_sums(0, w0)
    score_grads(0, w0, es0, PROMPT_CHUNKS)
    key_grads(0, PROMPT_CHUNKS)
    mate_copy(1, 1).start()
    prompt_arrived(0, 1)
    scores(1, PROMPT_CHUNKS, tops[1], sums[1])
    w1 = weights(1, tops[1], sums[1])
    send_plane(0, 1)
    mix(1, w1)
    send_plane(1, 1)
    prompt_arrived(1, 1)
    forward(1)
    value_grads(1, PROMPT_CHUNKS)
    mate_copy(2, 1).start()
    es1 = row_sums(1, w1)
    score_grads(1, w1, es1, PROMPT_CHUNKS)
    key_grads(1, PROMPT_CHUNKS)
    mate_copy(3, 1).start()
    send_plane(2, 1)
    score_grads(1, w1, es1, COMP_CHUNKS)
    send_plane(3, 1)
    score_grads(0, w0, es0, COMP_CHUNKS)

    def hand_out(packed, out):
        for b in range(8):
            bits = [packed[h, b * 64 : (b + 1) * 64, half(i)] for h in range(2) for i in range(2)]
            out[b * 256 : (b + 1) * 256, :] = nn(together, jnp.concatenate(bits, axis=0)).astype(BF16)

    for h in range(2):
        value_grads(h, COMP_CHUNKS)
    for h in range(2):
        key_grads(h, COMP_CHUNKS)
    for h in range(2):
        turn(kn, kT, h, 0, 512)
        query_grads(h)
    send_z(0, 1)
    hand_out(gv, value_out)
    send_z(1, 1)
    hand_out(gk, key_out)
    hand_out(gq, query_out)
    send_z(2, 1)
    send_z(3, 1)

    for which in range(2):
        for h in range(2):
            prompt_all(which, h).wait_send()
            forward_copy(which, h).wait_send()
    for group in GROUPS:
        mate_copy(*group).wait_send()
        plane_all(*group).wait_send()
    rows, cols = iota((32, 32), 0), iota((32, 32), 1)
    in_place = one_hot(cols == lax.rem(rows, 2) * 16 + lax.rem(lax.div(rows, 2), 8) * 2 + lax.div(rows, 16))
    z_all(0, 1).wait()
    z_all(2, 1).wait()
    pvalue_out[...] = nn(in_place, jnp.concatenate([sum_z(0), sum_z(2)], axis=0)).astype(BF16)
    z_all(1, 1).wait()
    first_key = sum_z(1)
    z_all(3, 1).wait()
    pkey_out[...] = nn(in_place, jnp.concatenate([first_key, sum_z(3)], axis=0)).astype(BF16)


def writer(*refs):
    ins, outs, sem = refs[:5], refs[5:10], refs[10]
    stores = [pltpu.make_async_copy(src, dst, sem.at[i]) for i, (src, dst) in enumerate(zip(ins, outs))]
    for store in stores:
        store.start()
    for store in stores:
        store.wait()


def interleaved(a):
    return a.reshape(512, 2, 2, 128).transpose(0, 2, 1, 3).reshape(2048, 128)


def by_token(a):
    return a.reshape(512, 2, 2, 128).transpose(0, 2, 1, 3).reshape(1, 512, 2, 256)


def shards(query, key, value, prompt_key, prompt_value, lam, gain, cotangent, lengths):
    vm = pltpu.VMEM
    dma = pltpu.SemaphoreType.DMA
    shape = jax.ShapeDtypeStruct
    anywhere = pl.BlockSpec(memory_space=pltpu.HBM)
    results = [((2048, 128), BF16)] * 3 + [((32, 256), BF16)] * 2
    held = pl.pallas_call(
        kernel,
        out_shape=[vm(*result) for result in results],
        in_specs=[anywhere] * 9,
        out_specs=[pl.BlockSpec(memory_space=vm)] * 5,
        scratch_shapes=[vm((2048, 128), BF16)] * 4
        + [vm((1024, 256), BF16)] * 2
        + [pltpu.SMEM((2,), F32), vm((2, 256), F32), pltpu.SMEM((1,), jnp.int32)]
        + [
            vm((2, 8, 2, 2, 32, 256), BF16),
            vm((2, 16, 2, 32, 256), BF16),
            vm((2, 16, 2, 32, 256), BF16),
            vm((2, 512, 256), BF16),
            vm((2, 512, 256), BF16),
            vm((2, 256, 1024), BF16),
            vm((2, 512, 256), F32),
            vm((2, 1024, 512), F32),
            vm((2, 1024, 512), F32),
            vm((2, 1024, 512), F32),
            vm((2, 1024, 512), BF16),
            vm((2, 1024, 512), BF16),
            vm((2, 1024, 512), BF16),
            vm((2, 512, 256), BF16),
            vm((2, 512, 256), BF16),
            vm((2, 512, 256), BF16),
            vm((2, 512, 256), BF16),
            vm((4, 2, 16, 16, 256), BF16),
            vm((4, 16, 16, 256), BF16),
            vm((4, 2, 8, 16, 256), BF16),
            vm((4, 2, 8, 16, 256), BF16),
            vm((4, 8, 16, 256), BF16),
            vm((4, 8, 16, 256), BF16),
        ]
        + [dma((15,)), dma((2, 2)), dma((2, 2)), dma((2, 2)), dma((2, 2))]
        + [dma((4,)), dma((4,)), dma((4,)), dma((4,)), dma((4,)), dma((4,))],
        compiler_params=pltpu.CompilerParams(
            collective_id=0, has_side_effects=True, vmem_limit_bytes=62 * 2**20
        ),
    )(
        interleaved(query), interleaved(key), interleaved(value), interleaved(cotangent),
        prompt_key.reshape(1024, 256), prompt_value.reshape(1024, 256), lam, gain, lengths,
    )
    outs = pl.pallas_call(
        writer,
        out_shape=[shape(*result) for result in results],
        in_specs=[pl.BlockSpec(memory_space=vm)] * 5,
        out_specs=[anywhere] * 5,
        scratch_shapes=[dma((5,))],
        compiler_params=pltpu.CompilerParams(vmem_limit_bytes=2 * 2**20),
    )(*held)
    return (
        by_token(outs[0]), by_token(outs[1]), by_token(outs[2]),
        outs[3].reshape(2, 16, 256), outs[4].reshape(2, 16, 256),
    )


def solution(mesh):
    heads = P("comp", None, "seq", None)
    in_specs = (
        heads, heads, heads, P("seq", None, None), P("seq", None, None), P("seq"), P("seq", None), heads, P("comp"),
    )
    owners = P(("comp", "seq"), None, None)
    return jax.shard_map(
        shards, mesh=mesh, in_specs=in_specs, out_specs=(heads, heads, heads, owners, owners), check_vma=False
    )
```
